128 devices in a mesh: ctx: 32 (over z, x, y_lo), dp: 4 (over y_hi, core).
Axes of the slice: x: 4, y: 4 (y_hi: 2, y_lo: 2; y = y_hi * 2 + y_lo), z: 4, core: 2. Of those that a mesh axis runs over, the one named last changes fastest.
Arguments:
- q_latent: bfloat16 [8192, 1536], P(('ctx', 'dp')), may hold values from -600 to 600
- kv_latent: bfloat16 [8192, 512], P(('ctx', 'dp')), may hold values from -6 to 6
- key_rope: bfloat16 [8192, 64], P(('ctx', 'dp')), may hold values from -6 to 6
- block_order: int32 [64], replicated, may hold values from 0 to 63, as said below
- w_query: bfloat16 [1536, 6144], P(None, 'dp'), may hold values from -16 to 16
- w_key: bfloat16 [512, 4096], P(None, 'dp'), may hold values from -6 to 6
- w_value: bfloat16 [512, 4096], P(None, 'dp'), may hold values from -6 to 6
- grad_query: bfloat16 [8192, 6144], P('ctx', 'dp'), may hold values from -6 to 6
- grad_key: bfloat16 [8192, 4096], P('ctx', 'dp'), may hold values from -6 to 6
- mom_query: float32 [1536, 6144], P('ctx', 'dp'), may hold values from -7240.7734 to 7240.7734
- mom_key: float32 [512, 4096], P('ctx', 'dp'), may hold values from -7240.7734 to 7240.7734
- clip_flags: int32 [32], P('dp'), may hold values 0 or 1
Outputs:
- attn_out: bfloat16 [8192, 4096], P('ctx', 'dp')
- max_logits: float32 [32], P('dp')
- step_query: float32 [1536, 6144], P('ctx', 'dp')
- step_key: float32 [512, 4096], P('ctx', 'dp')
- new_query: float32 [1536, 6144], P('ctx', 'dp')
- new_key: float32 [512, 4096], P('ctx', 'dp')
The draws below stay inside these ranges and needn't reach their ends.
Inputs may be any that keep to these rules, and one draw needn't show every extreme that they name: `block_order`: a permutation of 0 to 63 in which entries 2c and 2c + 1 sum to 63.
All inputs are finite; a program needn't handle non-finite values. No bound on the sum of `clip_flags` on one device may be relied on, other than what follows from the above.
Results may differ from the reference program's by a relative error of at most 0.013.
The reference program's roundings to bfloat16 on the way count: a program that leaves them out, or rounds other values in their place, can miss the bound.
Values may be sent and summed in bfloat16 or wider, within the bound.
No kernel may reach another device: no remote copies, remote signals or barrier semaphores. Data moves between devices by JAX's collectives and lax.ppermute only.
A program may use at most 128 MiB of HBM per device.

```python
import math
import jax
import jax.numpy as jnp
from jax import lax

QR = 1536
KVR = 512
NOPE = 128
ROPE = 64
VDIM = 128
HEADS = 32
NS_STEPS = 3
SEQ = 8192
HALF = 128
BLOCKS = 64


def draw_q_latent(key, part):
    values = jnp.clip(jax.random.normal(jax.random.fold_in(key, 11), (SEQ, QR), jnp.float32), -6.0, 6.0)
    return values.astype(jnp.bfloat16)


def draw_w_query(key, part):
    head_scale = jnp.exp(jax.random.uniform(jax.random.fold_in(key, 21), (1, HEADS, 1), jnp.float32, minval=math.log(0.5), maxval=math.log(2.5)))
    values = jnp.clip(jax.random.normal(jax.random.fold_in(key, 22), (QR, HEADS, NOPE + ROPE), jnp.float32), -6.0, 6.0)
    return (values * head_scale).reshape(QR, HEADS * (NOPE + ROPE)).astype(jnp.bfloat16)


def draw_block_order(key, part):
    first_blocks = jax.random.permutation(jax.random.fold_in(key, 31), BLOCKS // 2).astype(jnp.int32)
    flipped = jax.random.randint(jax.random.fold_in(key, 32), (BLOCKS // 2,), 0, 2).astype(jnp.int32)
    mirror_blocks = (BLOCKS - 1 - first_blocks).astype(jnp.int32)
    leading = jnp.where(flipped == 1, mirror_blocks, first_blocks)
    trailing = jnp.where(flipped == 1, first_blocks, mirror_blocks)
    return jnp.stack([leading, trailing], axis=1).reshape(BLOCKS).astype(jnp.int32)


def rising_momentum(key, row_count, column_count, top_ratio):
    level = jnp.arange(row_count, dtype=jnp.float32) / float(max(row_count - 1, 1))
    jitter = jax.random.uniform(jax.random.fold_in(key, 1), (row_count, 1), jnp.float32, minval=-0.3, maxval=0.3)
    row_scale = jnp.exp(level[:, None] * math.log(top_ratio) + jitter)
    values = jnp.clip(jax.random.normal(jax.random.fold_in(key, 2), (row_count, column_count), jnp.float32), -6.0, 6.0)
    return (values * row_scale * SEQ ** 0.5).astype(jnp.float32)


def draw_mom_query(key, part):
    key = jax.random.fold_in(key, 41)
    return rising_momentum(key, QR, HEADS * (NOPE + ROPE), 8.0)


def draw_mom_key(key, part):
    key = jax.random.fold_in(key, 51)
    return rising_momentum(key, KVR, HEADS * NOPE, 8.0)


def set_ends(array, stream_key, low, high):
    shape = array.shape
    spot = [jax.random.randint(jax.random.fold_in(stream_key, axis), (), 0, shape[axis]) for axis in range(len(shape))]
    array = array.at[tuple(spot)].set(low)
    longest = shape.index(max(shape))
    spot[longest] = (spot[longest] + 1) % shape[longest]
    return array.at[tuple(spot)].set(high)


def level_of(stream_key, shape, split, smallest, high):
    gain = 1.0
    for position, blocks in split:
        steps = jax.random.uniform(jax.random.fold_in(jax.random.fold_in(stream_key, 6), position), (blocks,), jnp.float32, smallest / len(split), high / len(split))
        gain = gain * jnp.repeat(jnp.exp(steps), shape[position] // blocks).reshape((-1,) + (1,) * (len(shape) - 1 - position))
    return gain


def noise(own_key, extent, spread, most, pieces=(), held_as=jnp.bfloat16):
    loudness = level_of(own_key, extent, pieces, -0.22, 0.18) if pieces else 1.0
    drawn = jax.random.normal(own_key, extent, jnp.float32) * spread * loudness
    return jnp.minimum(jnp.maximum(drawn, -most), most).astype(held_as)


def setup_inputs(seed: int = 0) -> dict:
    splits = jax.random.split(jax.random.key(seed), 13)
    return {
        "q_latent": draw_q_latent(jax.random.fold_in(splits[12], 71), 0),
        "kv_latent": noise(splits[1], (SEQ, KVR), 1.0, 6.0, ((0, 128),)),
        "key_rope": noise(splits[2], (SEQ, ROPE), 1.0, 6.0, ((0, 128),)),
        "block_order": draw_block_order(jax.random.fold_in(splits[12], 71), 0),
        "w_query": draw_w_query(jax.random.fold_in(splits[12], 71), 0),
        "w_key": noise(splits[5], (KVR, HEADS * NOPE), 1.0, 6.0, ((1, 4),)),
        "w_value": noise(splits[6], (KVR, HEADS * VDIM), 1.0, 6.0, ((1, 4),)),
        "grad_query": noise(splits[7], (SEQ, HEADS * (NOPE + ROPE)), 1.0, 6.0, ((0, 32), (1, 4))),
        "grad_key": noise(splits[8], (SEQ, HEADS * NOPE), 1.0, 6.0, ((0, 32), (1, 4))),
        "mom_query": draw_mom_query(jax.random.fold_in(splits[12], 71), 0),
        "mom_key": draw_mom_key(jax.random.fold_in(splits[12], 71), 0),
        "clip_flags": set_ends((jax.random.randint(splits[11], (HEADS,), 0, 2) < 1).astype(jnp.int32), jax.random.fold_in(splits[11], 1), 0, 1),
    }


NS_A = 3.4445
NS_B = -4.775
NS_C = 2.0315
MOMENTUM = 0.95
LEARN_RATE = 0.05
DECAY = 0.1
CLIP_TAU = 6.0
ROPE_THETA = 50000.0
FULL_PRECISION = lax.Precision.HIGHEST

def layout_positions(block_order):
    layout_rows = jnp.arange(SEQ, dtype=jnp.int32)
    return block_order[layout_rows // HALF] * HALF + layout_rows % HALF

def rotate_rope(rope_part, positions):
    pair_count = ROPE // 2
    frequency = ROPE_THETA ** (-2.0 * jnp.arange(pair_count, dtype=jnp.float32) / ROPE)
    angles = positions.astype(jnp.float32)[:, None] * frequency[None, :]
    cosine = jnp.cos(angles)
    sine_part = jnp.sin(angles)
    first_half = rope_part[..., :pair_count]
    second_half = rope_part[..., pair_count:]
    return jnp.concatenate([first_half * cosine - second_half * sine_part, second_half * cosine + first_half * sine_part], axis=-1)

def orthogonalize(moment, column_count):
    row_count = moment.shape[0]
    matrices = moment.reshape(row_count, -1, column_count).transpose(1, 0, 2)
    frob_norm = jnp.sqrt(lax.optimization_barrier(jnp.sum(matrices * matrices, axis=(1, 2))))
    iterate = matrices / (frob_norm[:, None, None] + 1e-07)
    for iteration in range(NS_STEPS):
        gram_matrix = jnp.einsum('hrc,hrd->hcd', iterate, iterate, precision=FULL_PRECISION)
        polynomial = NS_B * gram_matrix + NS_C * jnp.einsum('hcd,hde->hce', gram_matrix, gram_matrix, precision=FULL_PRECISION)
        iterate = NS_A * iterate + jnp.einsum('hrc,hcd->hrd', iterate, polynomial, precision=FULL_PRECISION)
    iterate = iterate * (0.2 * math.sqrt(row_count))
    return iterate.transpose(1, 0, 2).reshape(row_count, -1)

def reference(q_latent, kv_latent, key_rope, block_order, w_query, w_key, w_value, grad_query, grad_key, mom_query, mom_key, clip_flags):
    head_width = NOPE + ROPE
    score_scale = head_width ** (-0.5)
    positions = layout_positions(block_order)
    queries = jnp.dot(q_latent, w_query, preferred_element_type=jnp.float32) * QR ** (-0.5)
    queries = queries.reshape(SEQ, HEADS, head_width)
    query_nope = jnp.transpose(queries[:, :, :NOPE], (1, 0, 2)).astype(jnp.bfloat16)
    query_rope = rotate_rope(jnp.transpose(queries[:, :, NOPE:], (1, 0, 2)), positions).astype(jnp.bfloat16)
    key_heads = w_key.reshape(KVR, HEADS, NOPE).transpose(1, 0, 2)
    value_heads = w_value.reshape(KVR, HEADS, VDIM).transpose(1, 0, 2)
    allowed = positions[None, :] <= positions[:, None]

    def one_head(operands):
        nope_part, rotary_part, key_weight, value_weight = operands
        absorbed = (jnp.dot(nope_part, key_weight.T, preferred_element_type=jnp.float32) * KVR ** (-0.5)).astype(jnp.bfloat16)
        scores = jnp.dot(absorbed, kv_latent.T, preferred_element_type=jnp.float32)
        scores = (scores + jnp.dot(rotary_part, key_rope.T, preferred_element_type=jnp.float32)) * score_scale
        scores = jnp.where(allowed, scores, -jnp.inf)
        rowmax = lax.optimization_barrier(jnp.max(scores, axis=1))
        exp_terms = jnp.exp(scores - rowmax[:, None])
        row_total = lax.optimization_barrier(jnp.sum(exp_terms, axis=1))
        latent_out = (jnp.dot(exp_terms.astype(jnp.bfloat16), kv_latent, preferred_element_type=jnp.float32) / row_total[:, None]).astype(jnp.bfloat16)
        head_out = (jnp.dot(latent_out, value_weight, preferred_element_type=jnp.float32) * KVR ** (-0.5)).astype(jnp.bfloat16)
        return (head_out, jnp.max(rowmax))
    head_outputs, head_peaks = lax.map(one_head, (query_nope, query_rope, key_heads, value_heads))
    attn_out = head_outputs.transpose(1, 0, 2).reshape(SEQ, HEADS * VDIM)
    grad_q = jnp.dot(q_latent.T, grad_query, preferred_element_type=jnp.float32)
    grad_k = jnp.dot(kv_latent.T, grad_key, preferred_element_type=jnp.float32)
    moment_q = MOMENTUM * mom_query + grad_q
    moment_k = MOMENTUM * mom_key + grad_k
    step_query = orthogonalize(moment_q, head_width)
    step_key = orthogonalize(moment_k, NOPE)
    clip_gamma = jnp.where(clip_flags > 0, CLIP_TAU / jnp.maximum(head_peaks, CLIP_TAU), 1.0)
    root_gamma = jnp.sqrt(clip_gamma)
    query_factor = jnp.concatenate([jnp.broadcast_to(root_gamma[:, None], (HEADS, NOPE)), jnp.broadcast_to(clip_gamma[:, None], (HEADS, ROPE))], axis=1).reshape(-1)
    key_factor = jnp.repeat(root_gamma, NOPE)
    new_query = (w_query.astype(jnp.float32) * (1.0 - LEARN_RATE * DECAY) - LEARN_RATE * step_query) * query_factor[None, :]
    new_key = (w_key.astype(jnp.float32) * (1.0 - LEARN_RATE * DECAY) - LEARN_RATE * step_key) * key_factor[None, :]
    return (attn_out, head_peaks, step_query, step_key, new_query, new_key)
```

```python
import functools
import math

import jax
import jax.numpy as jnp
from jax import lax
from jax.experimental import pallas as pl
from jax.experimental.pallas import tpu as pltpu
from jax.sharding import Mesh
from jax.sharding import PartitionSpec as P

QR = 1536
KVR = 512
NOPE = 128
ROPE = 64
WIDE = 640
NS_STEPS = 3
NS_A = 3.4445
NS_B = -4.775
NS_C = 2.0315
MOMENTUM = 0.95
LEARN_RATE = 0.05
DECAY = 0.1
CLIP_TAU = 6.0
ROPE_THETA = 50000.0
HEAD = NOPE + ROPE
SCALE = HEAD ** (-0.5)
LOG2E = math.log2(math.e)
FULL = lax.Precision.HIGHEST
F32 = jnp.float32
BF16 = jnp.bfloat16
LOW = -1e30
ANY = pl.BlockSpec(memory_space=pl.ANY)
VMEM = pl.BlockSpec(memory_space=pltpu.VMEM)
SMEM = pl.BlockSpec(memory_space=pltpu.SMEM)
TILE = 512


def shift_first(k):
    pairs = []
    for z in range(4):
        for x in range(4):
            pairs.append(((z * 4 + x) * 2, (((z + k) % 4) * 4 + x) * 2))
            pairs.append(((z * 4 + x) * 2 + 1, (z * 4 + (x + k) % 4) * 2 + 1))
    return pairs


def shift_second(k):
    pairs = []
    for z in range(4):
        for x in range(4):
            pairs.append(((z * 4 + x) * 2, (z * 4 + (x + k) % 4) * 2))
            pairs.append(((z * 4 + x) * 2 + 1, (((z + k) % 4) * 4 + x) * 2 + 1))
    return pairs


def move_first(value, k):
    return lax.ppermute(value, ("z", "x", "c"), shift_first(k))


def move_second(value, k):
    return lax.ppermute(value, ("z", "x", "c"), shift_second(k))


def move_z(value, k):
    return lax.ppermute(value, "z", [(i, (i + k) % 4) for i in range(4)])


def flip(value, k):
    pairs = []
    for yl in range(2):
        for yh in range(2):
            pairs.append((yl * 2 + yh, (yl ^ (k & 1)) * 2 + (yh ^ (k >> 1))))
    return lax.ppermute(value, ("yl", "yh"), pairs)


def swap_core(value):
    return lax.ppermute(value, "c", [(0, 1), (1, 0)])


def attention_kernel(count_ref, place_ref, spos_ref, qpos_ref, q_ref, wv_ref, *rest):
    pieces = rest[:8]
    out_ref, peak_ref = rest[8:10]
    keys, acc, top, total, sem = rest[10:]
    for side in range(2):
        for part in range(4):
            piece = pieces[side * 4 + part]

            @pl.loop(0, 16)
            def _(s, piece=piece, side=side, part=part):
                row = pl.multiple_of(place_ref[side * 64 + part * 16 + s], 64)
                pltpu.make_async_copy(piece.at[s], keys.at[pl.ds(row, 64)], sem).start()

    pltpu.make_async_copy(keys, keys, sem).wait()
    factor = SCALE * LOG2E
    for half in range(2):
        top[...] = jnp.full(top.shape, LOW, F32)
        total[...] = jnp.zeros(total.shape, F32)
        acc[...] = jnp.zeros(acc.shape, F32)
        tiles = lax.div(count_ref[half] + 3, 4)

        def tile(j, masked, half=half):
            row0 = pl.multiple_of(j * TILE, TILE)
            for chunk in range(4):
                rows = pl.ds(chunk * 256, 256)
                q = q_ref[half, rows, :]
                k = keys[pl.ds(row0, TILE), :]
                s = lax.dot_general(q, k, (((1,), (1,)), ((), ())), preferred_element_type=F32)
                if masked:
                    row_pos = qpos_ref[half] * 128 + (
                        lax.broadcasted_iota(jnp.int32, (256, 128), 0) & 127
                    )
                    col = lax.broadcasted_iota(jnp.int32, (256, 128), 1)
                    parts = []
                    for b in range(4):
                        ok = spos_ref[j * 4 + b] * 128 + col <= row_pos
                        parts.append(jnp.where(ok, s[:, b * 128 : (b + 1) * 128], LOW))
                    s = jnp.concatenate(parts, axis=1)
                old = top[rows, :]
                new = jnp.maximum(old, jnp.max(s, axis=1, keepdims=True))
                p = jnp.exp2((s - new[:, :1]) * factor)
                keep = jnp.exp2((old - new) * factor)
                top[rows, :] = new
                total[rows, :] = total[rows, :] * keep + jnp.sum(p, axis=1, keepdims=True)
                acc[rows, :] = acc[rows, :] * keep[:, :1] + jnp.dot(
                    p.astype(BF16), k[:, :KVR], preferred_element_type=F32
                )

        @pl.loop(0, tiles - 1)
        def _(j):
            tile(j, False)

        tile(tiles - 1, True)
        for h in range(8):
            rows = pl.ds(h * 128, 128)
            latent = (acc[rows, :] / total[rows, :1]).astype(BF16)
            o = jnp.dot(latent, wv_ref[:, h * 128 : (h + 1) * 128], preferred_element_type=F32)
            out_ref[half * 128 : (half + 1) * 128, h * 128 : (h + 1) * 128] = (
                o * KVR ** (-0.5)
            ).astype(BF16)
            peak = jnp.max(top[rows, :], axis=0, keepdims=True) * SCALE
            if half == 0:
                peak_ref[h : h + 1, :] = peak
            else:
                peak_ref[h : h + 1, :] = jnp.maximum(peak_ref[h : h + 1, :], peak)


def attention(count, place, spos, qpos, queries, w_value, pieces):
    return pl.pallas_call(
        attention_kernel,
        out_shape=(
            jax.ShapeDtypeStruct((256, 1024), BF16),
            jax.ShapeDtypeStruct((8, 128), F32),
        ),
        in_specs=[SMEM] * 4 + [VMEM] * 2 + [ANY] * 8,
        out_specs=(VMEM, VMEM),
        scratch_shapes=[
            pltpu.VMEM((8192, WIDE), BF16),
            pltpu.VMEM((1024, KVR), F32),
            pltpu.VMEM((1024, 128), F32),
            pltpu.VMEM((1024, 128), F32),
            pltpu.SemaphoreType.DMA,
        ],
        compiler_params=pltpu.CompilerParams(vmem_limit_bytes=48 * 2**20),
        cost_estimate=pl.CostEstimate(
            flops=20 * 10**9, bytes_accessed=14 * 2**20, transcendentals=9 * 10**6
        ),
        name="attention",
    )(count, place, spos, qpos, queries, w_value, *pieces)


def gradient_kernel(zb_ref, xb_ref, g_own, g_other, l_own, l_other, *outs):
    for k in range(4):

        @pl.loop(0, 4)
        def _(j, k=k):
            zb = zb_ref[4 * k + j]
            xb = xb_ref[4 * k + j]

            def block(row0, height, col0, width):
                rows = pl.ds(pl.multiple_of(row0, 64), height)
                cols = pl.ds(pl.multiple_of(col0, 128), width)
                return jnp.dot(
                    g_own[rows, :], l_own[:, cols], preferred_element_type=F32
                ) + jnp.dot(g_other[rows, :], l_other[:, cols], preferred_element_type=F32)

            m = block(xb * HEAD, HEAD, zb * 384, 384)
            for t in range(3):
                outs[k][j, t * HEAD : (t + 1) * HEAD, :] = m[:, t * 128 : (t + 1) * 128]
            outs[k][j, 3 * HEAD : 704, :] = block(768 + xb * 128, 128, QR + zb * 128, 128)


def gradient_terms(zb, xb, g_own, g_other, l_own, l_other):
    return pl.pallas_call(
        gradient_kernel,
        out_shape=tuple(jax.ShapeDtypeStruct((4, 704, 128), F32) for _ in range(4)),
        in_specs=[SMEM] * 2 + [VMEM] * 4,
        out_specs=tuple(VMEM for _ in range(4)),
        compiler_params=pltpu.CompilerParams(vmem_limit_bytes=32 * 2**20),
        cost_estimate=pl.CostEstimate(
            flops=15 * 10**8, bytes_accessed=10 * 2**20, transcendentals=0
        ),
        name="gradient_terms",
    )(zb, xb, g_own, g_other, l_own, l_other)


def nt(a, b):
    return lax.dot_general(
        a, b, (((1,), (1,)), ((), ())), precision=FULL, preferred_element_type=F32
    )


def gram_kernel(a_ref, b_ref, c_ref, d_ref, mom_ref, m_ref, g_ref):
    m_ref[...] = (a_ref[...] + b_ref[...]) + (c_ref[...] + d_ref[...]) + MOMENTUM * mom_ref[...]
    g_ref[...] = jnp.zeros(g_ref.shape, F32)
    gram = None
    for t in range(3):
        block = m_ref[t * HEAD : (t + 1) * HEAD, :]
        term = nt(block, block)
        gram = term if gram is None else gram + term
    g_ref[:, :HEAD] = gram
    block = m_ref[3 * HEAD : 704, :]
    g_ref[:128, 256:384] = nt(block, block)


def moment_and_gram(parts, mom):
    return pl.pallas_call(
        gram_kernel,
        out_shape=(
            jax.ShapeDtypeStruct((704, 128), F32),
            jax.ShapeDtypeStruct((HEAD, 384), F32),
        ),
        in_specs=[VMEM] * 5,
        out_specs=(VMEM, VMEM),
        cost_estimate=pl.CostEstimate(
            flops=2 * 10**8, bytes_accessed=3 * 2**20, transcendentals=0
        ),
        name="moment_and_gram",
    )(*parts, mom)


def full_dot(a, b):
    return jnp.dot(a, b, precision=FULL, preferred_element_type=F32)


def newton_factor(gram):
    size = gram.shape[0]
    eye = (
        lax.broadcasted_iota(jnp.int32, (size, size), 0)
        == lax.broadcasted_iota(jnp.int32, (size, size), 1)
    ).astype(F32)
    square = jnp.sum(jnp.sum(gram * eye, axis=1, keepdims=True), axis=0, keepdims=True)
    inverse = 1.0 / (jnp.sqrt(square) + 1e-07)
    a = gram * inverse * inverse
    product = None
    for step in range(NS_STEPS):
        factor = NS_A * eye + NS_B * a + NS_C * full_dot(a, a)
        product = factor if product is None else full_dot(product, factor)
        if step + 1 < NS_STEPS:
            a = full_dot(full_dot(factor, a), factor)
    return product * inverse


def newton_kernel(m_ref, a_ref, b_ref, c_ref, d_ref, out_ref):
    gram = (a_ref[...] + b_ref[...]) + (c_ref[...] + d_ref[...])
    factor_q = newton_factor(gram[:, :HEAD]) * (0.2 * math.sqrt(QR))
    factor_k = newton_factor(gram[:128, 256:384]) * (0.2 * math.sqrt(KVR))
    rows = []
    for t in range(3):
        block = m_ref[t * HEAD : (t + 1) * HEAD, :]
        rows.append(
            lax.dot_general(
                block, factor_q, (((0,), (0,)), ((), ())), precision=FULL, preferred_element_type=F32
            )
        )
    step = jnp.concatenate(rows, axis=0)
    step_k = lax.dot_general(
        m_ref[3 * HEAD : 704, :],
        factor_k,
        (((0,), (0,)), ((), ())),
        precision=FULL,
        preferred_element_type=F32,
    )
    out_ref[...] = jnp.zeros(out_ref.shape, F32)
    for i in range(8):
        out_ref[i, :48, :HEAD] = step[i * 48 : (i + 1) * 48, :]
        out_ref[i, 48:, :128] = step_k[i * 16 : (i + 1) * 16, :]


def newton(moment, grams):
    return pl.pallas_call(
        newton_kernel,
        out_shape=jax.ShapeDtypeStruct((8, 64, 256), F32),
        in_specs=[VMEM] * 5,
        out_specs=VMEM,
        cost_estimate=pl.CostEstimate(
            flops=10**9, bytes_accessed=3 * 2**20, transcendentals=0
        ),
        name="newton",
    )(moment, *grams)


def rotate_rope(rope_part, positions):
    pair_count = ROPE // 2
    frequency = ROPE_THETA ** (-2.0 * jnp.arange(pair_count, dtype=F32) / ROPE)
    angles = positions.astype(F32)[:, None] * frequency[None, :]
    cosine = jnp.cos(angles)
    sine_part = jnp.sin(angles)
    first_half = rope_part[..., :pair_count]
    second_half = rope_part[..., pair_count:]
    return jnp.concatenate(
        [
            first_half * cosine - second_half * sine_part,
            second_half * cosine + first_half * sine_part,
        ],
        axis=-1,
    )


def look_up(table, index):
    hit = index[:, None] == jnp.arange(table.shape[0], dtype=jnp.int32)[None, :]
    return jnp.sum(jnp.where(hit, table[None, :], 0), axis=1)


def shards(
    q_latent,
    kv_latent,
    key_rope,
    block_order,
    w_query,
    w_key,
    w_value,
    grad_query,
    grad_key,
    mom_query,
    mom_key,
    clip_flags,
):
    z, x, c = lax.axis_index("z"), lax.axis_index("x"), lax.axis_index("c")
    yl, yh = lax.axis_index("yl"), lax.axis_index("yh")
    ctx = z * 8 + x * 2 + yl
    rows_in = jnp.concatenate(
        [q_latent, kv_latent, key_rope, jnp.zeros((64, 64), BF16)], axis=1
    )
    key_rows = rows_in[:, QR:]
    flips = [rows_in] + [flip(rows_in, k) for k in (1, 2, 3)]
    swapped = swap_core(jnp.stack(flips))
    shared = [
        [jnp.where(c == side, flips[k], swapped[k]) for side in range(2)] for k in range(4)
    ]

    def token_rows(low):
        halves = []
        for block in range(2):
            for side in range(2):
                halves.append(jnp.where(yh == block, shared[low][side], shared[low + 2][side]))
        return jnp.concatenate(halves, axis=0)

    l_own, l_other = token_rows(0), token_rows(1)
    grad_q_t = grad_query.T.reshape(2, 768, 256)
    grad_k_t = grad_key.T.reshape(2, 512, 256)

    def head_half(which):
        return jnp.concatenate(
            [
                jnp.where(which == 0, grad_q_t[0], grad_q_t[1]),
                jnp.where(which == 0, grad_k_t[0], grad_k_t[1]),
            ],
            axis=0,
        )

    g_own = head_half(yl)
    g_other = lax.ppermute(head_half(1 - yl), "yl", [(0, 1), (1, 0)])
    step_a = jnp.stack([key_rows] + [move_first(key_rows, k) for k in (1, 2, 3)])
    plane = jnp.stack([step_a] + [move_second(step_a, k) for k in (1, 2, 3)])
    plane = plane.reshape(16, 64, WIDE)
    mine = [plane] + [flip(plane, k) for k in (1, 2, 3)]
    theirs = [swap_core(piece) for piece in mine]
    mom_q = mom_query.reshape(48, 2, 4, HEAD).transpose(2, 1, 0, 3).reshape(8, 72, 128)
    mom_k = mom_key.reshape(16, 2, 4, 128).transpose(2, 1, 0, 3).reshape(8, 16, 128)
    mom = lax.all_to_all(jnp.concatenate([mom_q, mom_k], axis=1), ("x", "yl"), 0, 0)
    mom_q = mom[:, :72].reshape(3, 128, HEAD).transpose(0, 2, 1).reshape(576, 128)
    mom_k = mom[:, 72:].reshape(128, 128).T
    mom = jnp.concatenate([mom_q, mom_k], axis=0)
    k_index = jnp.arange(16, dtype=jnp.int32) // 4
    j_index = jnp.arange(16, dtype=jnp.int32) % 4
    zb = jnp.where(c == 0, z + k_index, z + j_index) % 4
    xb = jnp.where(c == 0, x + j_index, x + k_index) % 4
    terms = gradient_terms(zb, xb, g_own, g_other, l_own, l_other)
    stage = [terms[0]] + [move_first(terms[k], k) for k in (1, 2, 3)]
    sums = [(stage[0][j] + stage[1][j]) + (stage[2][j] + stage[3][j]) for j in range(4)]
    parts = [sums[0]] + [move_second(sums[k], k) for k in (1, 2, 3)]
    moment, gram = moment_and_gram(parts, mom)
    steps = newton(moment, [gram] + [move_z(gram, k) for k in (1, 2, 3)])
    steps = lax.all_to_all(steps, ("x", "yl"), 0, 0)
    step_query = (
        steps[:, :48, :HEAD].reshape(4, 2, 48, HEAD).transpose(2, 1, 0, 3).reshape(48, QR)
    )
    step_key = steps[:, 48:, :128].reshape(4, 2, 16, 128).transpose(2, 1, 0, 3).reshape(16, 1024)
    local_rows = jnp.arange(256, dtype=jnp.int32)
    qpos = look_up(block_order, 2 * ctx + jnp.arange(2, dtype=jnp.int32))
    query_pos = jnp.where(local_rows < 128, qpos[0], qpos[1]) * 128 + local_rows % 128
    queries = jnp.dot(l_own[:, :QR], w_query, preferred_element_type=F32) * QR ** (-0.5)
    queries = queries.reshape(256, 8, HEAD)
    query_nope = jnp.transpose(queries[:, :, :NOPE], (1, 0, 2)).astype(BF16)
    query_rope = rotate_rope(jnp.transpose(queries[:, :, NOPE:], (1, 0, 2)), query_pos).astype(
        BF16
    )
    absorbed = (
        jnp.einsum(
            "htn,khn->htk",
            query_nope,
            w_key.reshape(KVR, 8, NOPE),
            preferred_element_type=F32,
        )
        * KVR ** (-0.5)
    ).astype(BF16)
    wide = jnp.concatenate([absorbed, query_rope, jnp.zeros((8, 256, 64), BF16)], axis=2)
    wide = wide.reshape(8, 2, 128, WIDE).transpose(1, 0, 2, 3).reshape(2, 1024, WIDE)
    slot = jnp.arange(64, dtype=jnp.int32)
    part, b, a = slot // 16, (slot // 4) % 4, slot % 4
    part_yl, part_yh = (yl + part) % 2, (yh + part // 2) % 2

    def ranks(core):
        zz = jnp.where(core == 0, z - a, z - b) % 4
        xx = jnp.where(core == 0, x - b, x - a) % 4
        return look_up(block_order, 2 * (zz * 8 + xx * 2 + part_yl) + part_yh)

    place = jnp.concatenate([ranks(c) * 128 + c * 64, ranks(1 - c) * 128 + (1 - c) * 64])
    attn_out, peaks = attention(
        qpos + 1, place.astype(jnp.int32), slot, qpos, wide, w_value, mine + theirs
    )
    peaks = lax.all_to_all(jnp.broadcast_to(peaks[None], (32, 8, 128)), ("z", "x", "yl"), 0, 0)
    head_peaks = jnp.max(peaks, axis=0)[:, 0]
    clip_gamma = jnp.where(clip_flags > 0, CLIP_TAU / jnp.maximum(head_peaks, CLIP_TAU), 1.0)
    root_gamma = jnp.sqrt(clip_gamma)
    query_factor = jnp.concatenate(
        [
            jnp.broadcast_to(root_gamma[:, None], (8, NOPE)),
            jnp.broadcast_to(clip_gamma[:, None], (8, ROPE)),
        ],
        axis=1,
    ).reshape(-1)
    key_factor = jnp.repeat(root_gamma, NOPE)
    owned_query = lax.dynamic_slice_in_dim(w_query, ctx * 48, 48, 0).astype(F32)
    owned_key = lax.dynamic_slice_in_dim(w_key, ctx * 16, 16, 0).astype(F32)
    keep = 1.0 - LEARN_RATE * DECAY
    new_query = (owned_query * keep - LEARN_RATE * step_query) * query_factor[None, :]
    new_key = (owned_key * keep - LEARN_RATE * step_key) * key_factor[None, :]
    return (attn_out, head_peaks, step_query, step_key, new_query, new_key)


def solution(mesh):
    fine = Mesh(mesh.devices.reshape(4, 4, 2, 2, 2), ("z", "x", "yl", "yh", "c"))
    ctx, dp = ("z", "x", "yl"), ("yh", "c")
    tokens = P(ctx + dp, None)
    columns = P(None, dp)
    both = P(ctx, dp)
    in_specs = (
        tokens,
        tokens,
        tokens,
        P(),
        columns,
        columns,
        columns,
        both,
        both,
        both,
        both,
        P(dp),
    )
    out_specs = (both, P(dp), both, both, both, both)
    return jax.shard_map(shards, mesh=fine, in_specs=in_specs, out_specs=out_specs, check_vma=False)
```

```python
import functools
import math

import jax
import jax.numpy as jnp
from jax import lax
from jax.experimental import pallas as pl
from jax.experimental.pallas import tpu as pltpu
from jax.sharding import Mesh
from jax.sharding import PartitionSpec as P

QR = 1536
KVR = 512
NOPE = 128
ROPE = 64
WIDE = 640
NS_STEPS = 3
NS_A = 3.4445
NS_B = -4.775
NS_C = 2.0315
MOMENTUM = 0.95
LEARN_RATE = 0.05
DECAY = 0.1
CLIP_TAU = 6.0
ROPE_THETA = 50000.0
HEAD = NOPE + ROPE
SCALE = HEAD ** (-0.5)
LOG2E = math.log2(math.e)
FULL = lax.Precision.HIGHEST
F32 = jnp.float32
BF16 = jnp.bfloat16
LOW = -1e30
ANY = pl.BlockSpec(memory_space=pl.ANY)
VMEM = pl.BlockSpec(memory_space=pltpu.VMEM)
SMEM = pl.BlockSpec(memory_space=pltpu.SMEM)
TILE = 512


def place_of(z, x, c):
    return (z * 4 + x) * 2 + c


FOUR = range(4)
ALONG_Z = [[[place_of(z, x, c) for z in FOUR] for x in FOUR] for c in range(2)]
ALONG_X = [[[place_of(z, x, c) for x in FOUR] for z in FOUR] for c in range(2)]
FIRST = ALONG_Z[0] + ALONG_X[1]
SECOND = ALONG_X[0] + ALONG_Z[1]


def exchange(value, groups):
    return lax.all_to_all(value, ("z", "x", "c"), 0, 0, axis_index_groups=groups)


def move_z(value, k):
    return lax.ppermute(value, "z", [(i, (i + k) % 4) for i in range(4)])


def flip(value, k):
    pairs = []
    for yl in range(2):
        for yh in range(2):
            pairs.append((yl * 2 + yh, (yl ^ (k & 1)) * 2 + (yh ^ (k >> 1))))
    return lax.ppermute(value, ("yl", "yh"), pairs)


def swap_core(value):
    return lax.ppermute(value, "c", [(0, 1), (1, 0)])


def attention_kernel(head0, heads, count, *refs):
    place_ref, core_ref, qpos_ref, q_ref, wv_ref = refs[:5]
    pieces = refs[5 : 5 + count]
    out_ref, peak_ref, acc, top, total, keys, sem = refs[-7:]
    width = heads * 128
    slot = 0
    for index, piece in enumerate(pieces):
        side = 0 if index < count // 2 else 1
        if index == count // 2:
            slot = 0

        @pl.loop(0, piece.shape[0])
        def _(s, piece=piece, side=side, slot=slot):
            row = pl.multiple_of(place_ref[slot + s] * 128 + core_ref[side], 64)
            pltpu.make_async_copy(piece.at[s], keys.at[pl.ds(row, 64)], sem).start()

        slot += piece.shape[0]
    pltpu.make_async_copy(keys, keys, sem).wait()
    factor = SCALE * LOG2E
    for half in range(2):
        acc[...] = jnp.zeros(acc.shape, F32)
        top[...] = jnp.full(top.shape, LOW, F32)
        total[...] = jnp.zeros(total.shape, F32)
        tiles = lax.div(qpos_ref[half] + 4, 4)

        def tile(j, masked, half=half):
            row0 = pl.multiple_of(j * TILE, TILE)
            k = keys[pl.ds(row0, TILE), :]
            s = lax.dot_general(
                q_ref[half, head0 * 128 : head0 * 128 + width, :],
                k,
                (((1,), (1,)), ((), ())),
                preferred_element_type=F32,
            )
            s = [s[:, b * 128 : (b + 1) * 128] for b in range(4)]
            if masked:
                row_pos = qpos_ref[half] * 128 + (
                    lax.broadcasted_iota(jnp.int32, (width, 128), 0) & 127
                )
                col = lax.broadcasted_iota(jnp.int32, (width, 128), 1)
                s = [
                    jnp.where((j * 4 + b) * 128 + col <= row_pos, s[b], LOW) for b in range(4)
                ]
            old = top[...]
            peak = jnp.maximum(jnp.maximum(s[0], s[1]), jnp.maximum(s[2], s[3]))
            new = jnp.maximum(old, jnp.max(peak, axis=1, keepdims=True))
            p = [jnp.exp2((part - new) * factor) for part in s]
            keep = jnp.exp2((old - new) * factor)
            top[...] = new
            total[...] = total[...] * keep + ((p[0] + p[1]) + (p[2] + p[3]))
            weights = jnp.concatenate(p, axis=1).astype(BF16)
            acc[...] = acc[...] * jnp.concatenate([keep] * 4, axis=1) + jnp.dot(
                weights, k[:, :KVR], preferred_element_type=F32
            )

        @pl.loop(0, tiles - 1)
        def _(j):
            tile(j, False)

        tile(tiles - 1, True)
        for h in range(heads):
            rows = pl.ds(h * 128, 128)
            latent = acc[rows, :] / jnp.sum(total[rows, :], axis=1, keepdims=True)
            first = (head0 + h) * 128
            o = jnp.dot(
                latent.astype(BF16), wv_ref[:, first : first + 128], preferred_element_type=F32
            )
            out_ref[half * 128 : (half + 1) * 128, h * 128 : (h + 1) * 128] = (
                o * KVR ** (-0.5)
            ).astype(BF16)
            peak = jnp.max(top[rows, :], axis=0, keepdims=True) * SCALE
            if half == 0:
                peak_ref[h : h + 1, :] = peak
            else:
                peak_ref[h : h + 1, :] = jnp.maximum(peak_ref[h : h + 1, :], peak)


def attention(head0, heads, place, core_rows, qpos, queries, w_value, pieces, ties):
    width = heads * 128
    return pl.pallas_call(
        functools.partial(attention_kernel, head0, heads, len(pieces)),
        out_shape=(
            jax.ShapeDtypeStruct((256, width), BF16),
            jax.ShapeDtypeStruct((heads, 128), F32),
        ),
        in_specs=[SMEM] * 3 + [VMEM] * 2 + [ANY] * (len(pieces) + len(ties)),
        out_specs=(VMEM, VMEM),
        scratch_shapes=[
            pltpu.VMEM((width, KVR), F32),
            pltpu.VMEM((width, 128), F32),
            pltpu.VMEM((width, 128), F32),
            pltpu.VMEM((8192, WIDE), BF16),
            pltpu.SemaphoreType.DMA,
        ],
        compiler_params=pltpu.CompilerParams(vmem_limit_bytes=52 * 2**20),
        cost_estimate=pl.CostEstimate(
            flops=20 * heads // 8 * 10**9,
            bytes_accessed=14 * 2**20,
            transcendentals=heads * 10**6,
        ),
        name="attention",
    )(place, core_rows, qpos, queries, w_value, *pieces, *ties)


def query_kernel(l_ref, wq_ref, wk_ref, cos_ref, low_ref, high_ref, out_ref):
    for pair in range(4):
        both = (
            jnp.dot(
                l_ref[:, :QR],
                wq_ref[:, pair * 384 : (pair + 1) * 384],
                preferred_element_type=F32,
            )
            * QR ** (-0.5)
        )
        for odd in range(2):
            q = pltpu.roll(both, HEAD, 1) if odd else both
            h = 2 * pair + odd
            nope = q[:, :NOPE].astype(BF16)
            turn = q[:, NOPE : 2 * NOPE]
            turned = (
                turn * cos_ref[...]
                + pltpu.roll(turn, 96, 1) * low_ref[...]
                + pltpu.roll(turn, 32, 1) * high_ref[...]
            ).astype(BF16)
            absorbed = (
                lax.dot_general(
                    nope,
                    wk_ref[:, h * NOPE : (h + 1) * NOPE],
                    (((1,), (1,)), ((), ())),
                    preferred_element_type=F32,
                )
                * KVR ** (-0.5)
            ).astype(BF16)
            for half in range(2):
                rows = slice(half * 128, (half + 1) * 128)
                out_ref[half, h * 128 : (h + 1) * 128, :KVR] = absorbed[rows]
                out_ref[half, h * 128 : (h + 1) * 128, KVR:] = turned[rows]


def project_queries(l_own, w_query, w_key, cosine, low, high):
    return pl.pallas_call(
        query_kernel,
        out_shape=jax.ShapeDtypeStruct((2, 1024, WIDE), BF16),
        in_specs=[VMEM] * 6,
        out_specs=VMEM,
        compiler_params=pltpu.CompilerParams(vmem_limit_bytes=32 * 2**20),
        cost_estimate=pl.CostEstimate(flops=1000, bytes_accessed=1000, transcendentals=0),
        name="queries",
    )(l_own, w_query, w_key, cosine, low, high)


def gradient_kernel(at_ref, gq_ref, gk_ref, g_other, mq_ref, mk_ref, m_other, *rest):
    shards_own, shards_swapped = rest[:4], rest[4:8]
    out_ref, l_own, l_other, gq_t, gk_t, mq_t, mk_t = rest[-7:]
    core, z, x, yl, yh = (at_ref[i] for i in range(5))
    for k in range(4):
        target = l_other if k & 1 else l_own
        block = jnp.bitwise_xor(yh, k >> 1) * 128
        for side, shard in ((core, shards_own[k]), (1 - core, shards_swapped[k])):
            target[pl.ds(pl.multiple_of(block + side * 64, 64), 64), :] = shard[...]
    wide_q = pl.ds(pl.multiple_of(yl * 768, 128), 768)
    wide_k = pl.ds(pl.multiple_of(yl * 512, 128), 512)
    gq_t[0] = gq_ref[:, wide_q].T
    gk_t[0] = gk_ref[:, wide_k].T
    gq_t[1] = g_other[:, :768].T
    gk_t[1] = g_other[:, 768:].T

    def spread(own, other):
        low = jnp.where(yl == 0, own, other)
        high = jnp.where(yl == 0, other, own)
        pair = jnp.concatenate([low, high], axis=0)
        rows = [jnp.where(x == i, MOMENTUM, 0.0) * pair for i in range(4)]
        return jnp.concatenate(rows, axis=0).T

    mq_t[...] = spread(mq_ref[:, wide_q], m_other[:48, :])
    mk_t[...] = spread(mk_ref[:, wide_k], m_other[48:, :512])
    for zb in range(4):
        mine = jnp.where(z == zb, 1.0, 0.0)

        def block(g, cols):
            return jnp.dot(g[0], l_own[:, cols], preferred_element_type=F32) + jnp.dot(
                g[1], l_other[:, cols], preferred_element_type=F32
            )

        m = block(gq_t, slice(zb * 384, (zb + 1) * 384)) + mine * mq_t[...]
        mk = block(gk_t, slice(QR + zb * 128, QR + (zb + 1) * 128)) + mine * mk_t[...]
        for xb in range(4):
            k = jnp.where(core == 0, zb, xb)
            j = jnp.where(core == 0, xb, zb)
            for t in range(3):
                out_ref[k, j, t * HEAD : (t + 1) * HEAD, :] = m[
                    xb * HEAD : (xb + 1) * HEAD, t * 128 : (t + 1) * 128
                ]
            out_ref[k, j, 3 * HEAD : 704, :] = mk[xb * 128 : (xb + 1) * 128, :]


def gradient_terms(at, grad_query, grad_key, g_other, mom_query, mom_key, m_other, shards, ties):
    return pl.pallas_call(
        gradient_kernel,
        out_shape=(
            jax.ShapeDtypeStruct((4, 4, 704, 128), F32),
            jax.ShapeDtypeStruct((256, QR + WIDE), BF16),
        ),
        in_specs=[SMEM] + [VMEM] * 14 + [ANY] * len(ties),
        out_specs=(VMEM, VMEM),
        scratch_shapes=[
            pltpu.VMEM((256, QR + WIDE), BF16),
            pltpu.VMEM((2, 768, 256), BF16),
            pltpu.VMEM((2, 512, 256), BF16),
            pltpu.VMEM((768, 384), F32),
            pltpu.VMEM((512, 128), F32),
        ],
        compiler_params=pltpu.CompilerParams(vmem_limit_bytes=32 * 2**20),
        cost_estimate=pl.CostEstimate(flops=1000, bytes_accessed=1000, transcendentals=0),
        name="gradient_terms",
    )(at, grad_query, grad_key, g_other, mom_query, mom_key, m_other, *shards, *ties)


def sum_kernel(a_ref, *rest):
    rest[-1][0] = (a_ref[0, 0] + a_ref[1, 0]) + (a_ref[2, 0] + a_ref[3, 0])


def sum_first(terms, ties):
    return pl.pallas_call(
        sum_kernel,
        grid=(4,),
        out_shape=jax.ShapeDtypeStruct((4, 704, 128), F32),
        in_specs=[pl.BlockSpec((4, 1, 704, 128), lambda j: (0, j, 0, 0))] + [ANY] * len(ties),
        out_specs=pl.BlockSpec((1, 704, 128), lambda j: (j, 0, 0)),
        compiler_params=pltpu.CompilerParams(vmem_limit_bytes=16 * 2**20),
        cost_estimate=pl.CostEstimate(flops=1000, bytes_accessed=1000, transcendentals=0),
        name="sum_first",
    )(terms, *ties)


def nt(a, b):
    return lax.dot_general(
        a, b, (((1,), (1,)), ((), ())), precision=FULL, preferred_element_type=F32
    )


def gram_kernel(p_ref, peak_ref, m_ref, g_ref):
    m_ref[...] = (p_ref[0] + p_ref[1]) + (p_ref[2] + p_ref[3])
    g_ref[...] = jnp.zeros(g_ref.shape, F32)
    gram = None
    for t in range(3):
        block = m_ref[t * HEAD : (t + 1) * HEAD, :]
        term = nt(block, block)
        gram = term if gram is None else gram + term
    g_ref[:, :HEAD] = gram
    block = m_ref[3 * HEAD : 704, :]
    g_ref[:128, 256:384] = nt(block, block)
    g_ref[128:136, 256:384] = peak_ref[...]


def moment_and_gram(parts, peaks):
    return pl.pallas_call(
        gram_kernel,
        out_shape=(
            jax.ShapeDtypeStruct((704, 128), F32),
            jax.ShapeDtypeStruct((HEAD, 384), F32),
        ),
        in_specs=[VMEM, VMEM],
        out_specs=(VMEM, VMEM),
        cost_estimate=pl.CostEstimate(flops=1000, bytes_accessed=1000, transcendentals=0),
        name="moment_and_gram",
    )(parts, peaks)


def full_dot(a, b):
    return jnp.dot(a, b, precision=FULL, preferred_element_type=F32)


def newton_factor(gram):
    size = gram.shape[0]
    eye = (
        lax.broadcasted_iota(jnp.int32, (size, size), 0)
        == lax.broadcasted_iota(jnp.int32, (size, size), 1)
    ).astype(F32)
    square = jnp.sum(jnp.sum(gram * eye, axis=1, keepdims=True), axis=0, keepdims=True)
    inverse = 1.0 / (jnp.sqrt(square) + 1e-07)
    a = gram * inverse * inverse
    product = None
    for step in range(NS_STEPS):
        factor = NS_A * eye + NS_B * a + NS_C * full_dot(a, a)
        product = factor if product is None else full_dot(product, factor)
        if step + 1 < NS_STEPS:
            a = full_dot(full_dot(factor, a), factor)
    return product * inverse


def newton_kernel(m_ref, a_ref, b_ref, c_ref, d_ref, *rest):
    out_ref = rest[-1]
    spot = (slice(128, 136), slice(256, 384))
    peaks = jnp.maximum(
        jnp.maximum(a_ref[spot], b_ref[spot]), jnp.maximum(c_ref[spot], d_ref[spot])
    )
    gram = (a_ref[...] + b_ref[...]) + (c_ref[...] + d_ref[...])
    factor_q = newton_factor(gram[:, :HEAD]) * (0.2 * math.sqrt(QR))
    factor_k = newton_factor(gram[:128, 256:384]) * (0.2 * math.sqrt(KVR))
    rows = []
    for t in range(3):
        block = m_ref[t * HEAD : (t + 1) * HEAD, :]
        rows.append(
            lax.dot_general(
                block, factor_q, (((0,), (0,)), ((), ())), precision=FULL, preferred_element_type=F32
            )
        )
    step = jnp.concatenate(rows, axis=0)
    step_k = lax.dot_general(
        m_ref[3 * HEAD : 704, :],
        factor_k,
        (((0,), (0,)), ((), ())),
        precision=FULL,
        preferred_element_type=F32,
    )
    out_ref[...] = jnp.zeros(out_ref.shape, F32)
    for i in range(8):
        out_ref[i, :48, :HEAD] = step[i * 48 : (i + 1) * 48, :]
        out_ref[i, 48:, :128] = step_k[i * 16 : (i + 1) * 16, :]
        out_ref[i, 48:56, 128:] = peaks


def newton(moment, grams, ties):
    return pl.pallas_call(
        newton_kernel,
        out_shape=jax.ShapeDtypeStruct((8, 64, 256), F32),
        in_specs=[VMEM] * 5 + [ANY] * len(ties),
        out_specs=VMEM,
        cost_estimate=pl.CostEstimate(flops=1000, bytes_accessed=1000, transcendentals=0),
        name="newton",
    )(moment, *grams, *ties)


def turn_tables(positions):
    frequency = ROPE_THETA ** (-2.0 * jnp.arange(ROPE // 2, dtype=F32) / ROPE)
    angles = positions.astype(F32)[:, None] * frequency[None, :]
    cosine, sine = jnp.cos(angles), jnp.sin(angles)
    none = jnp.zeros_like(cosine)
    return (
        jnp.concatenate([cosine, cosine, none, none], axis=1),
        jnp.concatenate([-sine, none, none, none], axis=1),
        jnp.concatenate([none, sine, none, none], axis=1),
    )


def look_up(table, index):
    hit = index[:, None] == jnp.arange(table.shape[0], dtype=jnp.int32)[None, :]
    return jnp.sum(jnp.where(hit, table[None, :], 0), axis=1)


def shards(
    q_latent,
    kv_latent,
    key_rope,
    block_order,
    w_query,
    w_key,
    w_value,
    grad_query,
    grad_key,
    mom_query,
    mom_key,
    clip_flags,
):
    z, x, c = lax.axis_index("z"), lax.axis_index("x"), lax.axis_index("c")
    yl, yh = lax.axis_index("yl"), lax.axis_index("yh")
    ctx = z * 8 + x * 2 + yl
    rows_in = jnp.concatenate(
        [q_latent, kv_latent, key_rope, jnp.zeros((64, 64), BF16)], axis=1
    )
    key_rows = rows_in[:, QR:]
    flips = [rows_in] + [flip(rows_in, k) for k in (1, 2, 3)]
    swapped = [swap_core(piece) for piece in flips]

    def other_half(first, second):
        def pick(array):
            width = array.shape[1] // 2
            return jnp.where(yl == 0, array[:, width:], array[:, :width])

        return pick(first), pick(second)

    g_other = jnp.concatenate(other_half(grad_query, grad_key), axis=1)
    g_other = lax.ppermute(g_other, "yl", [(0, 1), (1, 0)])
    mom_q, mom_k = other_half(mom_query, mom_key)
    m_other = jnp.concatenate([mom_q, jnp.pad(mom_k, ((0, 0), (0, 256)))], axis=0)
    m_other = lax.ppermute(m_other, "yl", [(0, 1), (1, 0)])
    plane = lax.all_to_all(
        jnp.broadcast_to(key_rows[None], (16, 64, WIDE)), ("z", "x"), 0, 0
    )
    at = jnp.stack([c, z, x, yl, yh]).astype(jnp.int32)
    terms, l_own = gradient_terms(
        at, grad_query, grad_key, g_other, mom_query, mom_key, m_other, flips + swapped, [plane]
    )
    terms = exchange(terms, FIRST)
    near = [flip(plane, k) for k in (1, 3)]
    local_rows = jnp.arange(256, dtype=jnp.int32)
    qpos = look_up(block_order, 2 * ctx + jnp.arange(2, dtype=jnp.int32))
    query_pos = jnp.where(local_rows < 128, qpos[0], qpos[1]) * 128 + local_rows % 128
    wide = project_queries(l_own, w_query, w_key, *turn_tables(query_pos))
    after = wide[0, 0, WIDE - 1]
    far = [flip(near[1][:8] + after, 1), flip(near[0][8:] + after, 3)]
    slot = jnp.arange(16, dtype=jnp.int32)
    place = jnp.concatenate(
        [
            look_up(
                block_order,
                2 * (slot // 4 * 8 + slot % 4 * 2 + (yl ^ (k & 1))) + (yh ^ (k >> 1)),
            )
            for k in (0, 1, 3, 2)
        ]
    )
    core_rows = jnp.stack([c * 64, 64 - c * 64]).astype(jnp.int32)

    terms = sum_first(terms, [wide])
    later = (terms[0, 0, 0] * 0).astype(BF16)
    far = [piece + later for piece in far]
    mine = [plane, *near, *far]
    pieces = mine + [swap_core(piece) for piece in mine]
    parts = exchange(terms, SECOND)
    attn_out, peaks = attention(
        0, 8, place, core_rows, qpos, wide, w_value, pieces, []
    )
    moment, gram = moment_and_gram(parts, peaks)
    grams = [gram] + [move_z(gram, k) for k in (1, 2, 3)]
    steps = newton(moment, grams, [])
    steps = lax.all_to_all(steps, ("x", "yl"), 0, 0)
    step_query = (
        steps[:, :48, :HEAD].reshape(4, 2, 48, HEAD).transpose(2, 1, 0, 3).reshape(48, QR)
    )
    step_key = steps[:, 48:, :128].reshape(4, 2, 16, 128).transpose(2, 1, 0, 3).reshape(16, 1024)
    head_peaks = jnp.max(steps[:, 48:56, 128], axis=0)
    clip_gamma = jnp.where(clip_flags > 0, CLIP_TAU / jnp.maximum(head_peaks, CLIP_TAU), 1.0)
    root_gamma = jnp.sqrt(clip_gamma)
    query_factor = jnp.concatenate(
        [
            jnp.broadcast_to(root_gamma[:, None], (8, NOPE)),
            jnp.broadcast_to(clip_gamma[:, None], (8, ROPE)),
        ],
        axis=1,
    ).reshape(-1)
    key_factor = jnp.repeat(root_gamma, NOPE)
    owned_query = lax.dynamic_slice_in_dim(w_query, ctx * 48, 48, 0).astype(F32)
    owned_key = lax.dynamic_slice_in_dim(w_key, ctx * 16, 16, 0).astype(F32)
    keep = 1.0 - LEARN_RATE * DECAY
    new_query = (owned_query * keep - LEARN_RATE * step_query) * query_factor[None, :]
    new_key = (owned_key * keep - LEARN_RATE * step_key) * key_factor[None, :]
    return (attn_out, head_peaks, step_query, step_key, new_query, new_key)


def solution(mesh):
    fine = Mesh(mesh.devices.reshape(4, 4, 2, 2, 2), ("z", "x", "yl", "yh", "c"))
    ctx, dp = ("z", "x", "yl"), ("yh", "c")
    tokens = P(ctx + dp, None)
    columns = P(None, dp)
    both = P(ctx, dp)
    in_specs = (
        tokens,
        tokens,
        tokens,
        P(),
        columns,
        columns,
        columns,
        both,
        both,
        both,
        both,
        P(dp),
    )
    out_specs = (both, P(dp), both, both, both, both)
    return jax.shard_map(shards, mesh=fine, in_specs=in_specs, out_specs=out_specs, check_vma=False)
```

```python
import functools
import math

import jax
import jax.numpy as jnp
from jax import lax
from jax.experimental import pallas as pl
from jax.experimental.pallas import tpu as pltpu
from jax.sharding import Mesh
from jax.sharding import PartitionSpec as P

QR = 1536
KVR = 512
NOPE = 128
ROPE = 64
WIDE = 640
NS_STEPS = 3
NS_A = 3.4445
NS_B = -4.775
NS_C = 2.0315
MOMENTUM = 0.95
LEARN_RATE = 0.05
DECAY = 0.1
CLIP_TAU = 6.0
ROPE_THETA = 50000.0
HEAD = NOPE + ROPE
SCALE = HEAD ** (-0.5)
LOG2E = math.log2(math.e)
FULL = lax.Precision.HIGHEST
F32 = jnp.float32
BF16 = jnp.bfloat16
LOW = -1e30
ANY = pl.BlockSpec(memory_space=pl.ANY)
VMEM = pl.BlockSpec(memory_space=pltpu.VMEM)
SMEM = pl.BlockSpec(memory_space=pltpu.SMEM)
TILE = 512


def place_of(z, x, c):
    return (z * 4 + x) * 2 + c


FOUR = range(4)
ALONG_Z = [[[place_of(z, x, c) for z in FOUR] for x in FOUR] for c in range(2)]
ALONG_X = [[[place_of(z, x, c) for x in FOUR] for z in FOUR] for c in range(2)]
FIRST = ALONG_Z[0] + ALONG_X[1]
SECOND = ALONG_X[0] + ALONG_Z[1]


def exchange(value, groups):
    return lax.all_to_all(value, ("z", "x", "c"), 0, 0, axis_index_groups=groups)


def move_z(value, k):
    return lax.ppermute(value, "z", [(i, (i + k) % 4) for i in range(4)])


def flip(value, k):
    pairs = []
    for yl in range(2):
        for yh in range(2):
            pairs.append((yl * 2 + yh, (yl ^ (k & 1)) * 2 + (yh ^ (k >> 1))))
    return lax.ppermute(value, ("yl", "yh"), pairs)


def swap_core(value):
    return lax.ppermute(value, "c", [(0, 1), (1, 0)])


def attention_kernel(head0, heads, count, *refs):
    place_ref, core_ref, qpos_ref, q_ref, wv_ref = refs[:5]
    pieces = refs[5 : 5 + count]
    out_ref, peak_ref, acc, top, total, keys, sem = refs[-7:]
    width = heads * 128
    slot = 0
    for index, piece in enumerate(pieces):
        side = 0 if index < count // 2 else 1
        if index == count // 2:
            slot = 0

        @pl.loop(0, piece.shape[0])
        def _(s, piece=piece, side=side, slot=slot):
            row = pl.multiple_of(place_ref[slot + s] * 128 + core_ref[side], 64)
            pltpu.make_async_copy(piece.at[s], keys.at[pl.ds(row, 64)], sem).start()

        slot += piece.shape[0]
    pltpu.make_async_copy(keys, keys, sem).wait()
    factor = SCALE * LOG2E
    for half in range(2):
        acc[...] = jnp.zeros(acc.shape, F32)
        top[...] = jnp.full(top.shape, LOW, F32)
        total[...] = jnp.zeros(total.shape, F32)
        tiles = lax.div(qpos_ref[half] + 4, 4)

        def tile(j, masked, half=half):
            row0 = pl.multiple_of(j * TILE, TILE)
            k = keys[pl.ds(row0, TILE), :]
            s = lax.dot_general(
                q_ref[half, head0 * 128 : head0 * 128 + width, :],
                k,
                (((1,), (1,)), ((), ())),
                preferred_element_type=F32,
            )
            s = [s[:, b * 128 : (b + 1) * 128] for b in range(4)]
            if masked:
                row_pos = qpos_ref[half] * 128 + (
                    lax.broadcasted_iota(jnp.int32, (width, 128), 0) & 127
                )
                col = lax.broadcasted_iota(jnp.int32, (width, 128), 1)
                s = [
                    jnp.where((j * 4 + b) * 128 + col <= row_pos, s[b], LOW) for b in range(4)
                ]
            old = top[...]
            peak = jnp.maximum(jnp.maximum(s[0], s[1]), jnp.maximum(s[2], s[3]))
            new = jnp.maximum(old, jnp.max(peak, axis=1, keepdims=True))
            p = [jnp.exp2((part - new) * factor) for part in s]
            keep = jnp.exp2((old - new) * factor)
            top[...] = new
            total[...] = total[...] * keep + ((p[0] + p[1]) + (p[2] + p[3]))
            weights = jnp.concatenate(p, axis=1).astype(BF16)
            acc[...] = acc[...] * jnp.concatenate([keep] * 4, axis=1) + jnp.dot(
                weights, k[:, :KVR], preferred_element_type=F32
            )

        @pl.loop(0, tiles - 1)
        def _(j):
            tile(j, False)

        tile(tiles - 1, True)
        for h in range(heads):
            rows = pl.ds(h * 128, 128)
            latent = acc[rows, :] / jnp.sum(total[rows, :], axis=1, keepdims=True)
            first = (head0 + h) * 128
            o = jnp.dot(
                latent.astype(BF16), wv_ref[:, first : first + 128], preferred_element_type=F32
            )
            out_ref[half * 128 : (half + 1) * 128, h * 128 : (h + 1) * 128] = (
                o * KVR ** (-0.5)
            ).astype(BF16)
            peak = jnp.max(top[rows, :], axis=0, keepdims=True) * SCALE
            if half == 0:
                peak_ref[h : h + 1, :] = peak
            else:
                peak_ref[h : h + 1, :] = jnp.maximum(peak_ref[h : h + 1, :], peak)


def attention(head0, heads, place, core_rows, qpos, queries, w_value, pieces, ties):
    width = heads * 128
    return pl.pallas_call(
        functools.partial(attention_kernel, head0, heads, len(pieces)),
        out_shape=(
            jax.ShapeDtypeStruct((256, width), BF16),
            jax.ShapeDtypeStruct((heads, 128), F32),
        ),
        in_specs=[SMEM] * 3 + [VMEM] * 2 + [ANY] * (len(pieces) + len(ties)),
        out_specs=(VMEM, VMEM),
        scratch_shapes=[
            pltpu.VMEM((width, KVR), F32),
            pltpu.VMEM((width, 128), F32),
            pltpu.VMEM((width, 128), F32),
            pltpu.VMEM((8192, WIDE), BF16),
            pltpu.SemaphoreType.DMA,
        ],
        compiler_params=pltpu.CompilerParams(vmem_limit_bytes=52 * 2**20),
        cost_estimate=pl.CostEstimate(
            flops=20 * heads // 8 * 10**9,
            bytes_accessed=14 * 2**20,
            transcendentals=heads * 10**6,
        ),
        name="attention",
    )(place, core_rows, qpos, queries, w_value, *pieces, *ties)


def mark_kernel(*refs):
    refs[-1][...] = jnp.zeros((8, 128), F32)


def mark_after(ties):
    return pl.pallas_call(
        mark_kernel,
        out_shape=jax.ShapeDtypeStruct((8, 128), F32),
        in_specs=[ANY] * len(ties),
        out_specs=VMEM,
        compiler_params=pltpu.CompilerParams(vmem_limit_bytes=2**20),
        cost_estimate=pl.CostEstimate(flops=34 * 10**9, bytes_accessed=1000, transcendentals=0),
        name="mark",
    )(*ties)


def query_kernel(l_ref, wq_ref, wk_ref, cos_ref, low_ref, high_ref, out_ref):
    for pair in range(4):
        both = (
            jnp.dot(
                l_ref[:, :QR],
                wq_ref[:, pair * 384 : (pair + 1) * 384],
                preferred_element_type=F32,
            )
            * QR ** (-0.5)
        )
        for odd in range(2):
            q = pltpu.roll(both, HEAD, 1) if odd else both
            h = 2 * pair + odd
            nope = q[:, :NOPE].astype(BF16)
            turn = q[:, NOPE : 2 * NOPE]
            turned = (
                turn * cos_ref[...]
                + pltpu.roll(turn, 96, 1) * low_ref[...]
                + pltpu.roll(turn, 32, 1) * high_ref[...]
            ).astype(BF16)
            absorbed = (
                lax.dot_general(
                    nope,
                    wk_ref[:, h * NOPE : (h + 1) * NOPE],
                    (((1,), (1,)), ((), ())),
                    preferred_element_type=F32,
                )
                * KVR ** (-0.5)
            ).astype(BF16)
            for half in range(2):
                rows = slice(half * 128, (half + 1) * 128)
                out_ref[half, h * 128 : (h + 1) * 128, :KVR] = absorbed[rows]
                out_ref[half, h * 128 : (h + 1) * 128, KVR:] = turned[rows]


def project_queries(l_own, w_query, w_key, cosine, low, high):
    return pl.pallas_call(
        query_kernel,
        out_shape=jax.ShapeDtypeStruct((2, 1024, WIDE), BF16),
        in_specs=[VMEM] * 6,
        out_specs=VMEM,
        compiler_params=pltpu.CompilerParams(vmem_limit_bytes=32 * 2**20),
        cost_estimate=pl.CostEstimate(flops=1000, bytes_accessed=1000, transcendentals=0),
        name="queries",
    )(l_own, w_query, w_key, cosine, low, high)


def gradient_kernel(at_ref, gq_ref, gk_ref, g_other, mq_ref, mk_ref, m_other, *rest):
    shards_own, shards_swapped = rest[:4], rest[4:8]
    out_ref, l_own, l_other, gq_t, gk_t, mq_t, mk_t = rest[-7:]
    core, z, x, yl, yh = (at_ref[i] for i in range(5))
    for k in range(4):
        target = l_other if k & 1 else l_own
        block = jnp.bitwise_xor(yh, k >> 1) * 128
        for side, shard in ((core, shards_own[k]), (1 - core, shards_swapped[k])):
            target[pl.ds(pl.multiple_of(block + side * 64, 64), 64), :] = shard[...]
    wide_q = pl.ds(pl.multiple_of(yl * 768, 128), 768)
    wide_k = pl.ds(pl.multiple_of(yl * 512, 128), 512)
    gq_t[0] = gq_ref[:, wide_q].T
    gk_t[0] = gk_ref[:, wide_k].T
    gq_t[1] = g_other[:, :768].T
    gk_t[1] = g_other[:, 768:].T

    def spread(own, other):
        low = jnp.where(yl == 0, own, other)
        high = jnp.where(yl == 0, other, own)
        pair = jnp.concatenate([low, high], axis=0)
        rows = [jnp.where(x == i, MOMENTUM, 0.0) * pair for i in range(4)]
        return jnp.concatenate(rows, axis=0).T

    mq_t[...] = spread(mq_ref[:, wide_q], m_other[:48, :])
    mk_t[...] = spread(mk_ref[:, wide_k], m_other[48:, :512])
    for zb in range(4):
        mine = jnp.where(z == zb, 1.0, 0.0)

        def block(g, cols):
            return jnp.dot(g[0], l_own[:, cols], preferred_element_type=F32) + jnp.dot(
                g[1], l_other[:, cols], preferred_element_type=F32
            )

        m = block(gq_t, slice(zb * 384, (zb + 1) * 384)) + mine * mq_t[...]
        mk = block(gk_t, slice(QR + zb * 128, QR + (zb + 1) * 128)) + mine * mk_t[...]
        for xb in range(4):
            k = jnp.where(core == 0, zb, xb)
            j = jnp.where(core == 0, xb, zb)
            for t in range(3):
                out_ref[k, j, t * HEAD : (t + 1) * HEAD, :] = m[
                    xb * HEAD : (xb + 1) * HEAD, t * 128 : (t + 1) * 128
                ]
            out_ref[k, j, 3 * HEAD : 704, :] = mk[xb * 128 : (xb + 1) * 128, :]


def gradient_terms(at, grad_query, grad_key, g_other, mom_query, mom_key, m_other, shards, ties):
    return pl.pallas_call(
        gradient_kernel,
        out_shape=(
            jax.ShapeDtypeStruct((4, 4, 704, 128), F32),
            jax.ShapeDtypeStruct((256, QR + WIDE), BF16),
        ),
        in_specs=[SMEM] + [VMEM] * 14 + [ANY] * len(ties),
        out_specs=(VMEM, VMEM),
        scratch_shapes=[
            pltpu.VMEM((256, QR + WIDE), BF16),
            pltpu.VMEM((2, 768, 256), BF16),
            pltpu.VMEM((2, 512, 256), BF16),
            pltpu.VMEM((768, 384), F32),
            pltpu.VMEM((512, 128), F32),
        ],
        compiler_params=pltpu.CompilerParams(vmem_limit_bytes=56 * 2**20),
        cost_estimate=pl.CostEstimate(flops=1000, bytes_accessed=1000, transcendentals=0),
        name="gradient_terms",
    )(at, grad_query, grad_key, g_other, mom_query, mom_key, m_other, *shards, *ties)


def sum_kernel(a_ref, *rest):
    rest[-1][0] = (a_ref[0, 0] + a_ref[1, 0]) + (a_ref[2, 0] + a_ref[3, 0])


def sum_first(terms, ties):
    return pl.pallas_call(
        sum_kernel,
        grid=(4,),
        out_shape=jax.ShapeDtypeStruct((4, 704, 128), F32),
        in_specs=[pl.BlockSpec((4, 1, 704, 128), lambda j: (0, j, 0, 0))] + [ANY] * len(ties),
        out_specs=pl.BlockSpec((1, 704, 128), lambda j: (j, 0, 0)),
        compiler_params=pltpu.CompilerParams(vmem_limit_bytes=16 * 2**20),
        cost_estimate=pl.CostEstimate(flops=1000, bytes_accessed=1000, transcendentals=0),
        name="sum_first",
    )(terms, *ties)


def nt(a, b):
    return lax.dot_general(
        a, b, (((1,), (1,)), ((), ())), precision=FULL, preferred_element_type=F32
    )


def gram_kernel(p_ref, peak_ref, m_ref, g_ref):
    m_ref[...] = (p_ref[0] + p_ref[1]) + (p_ref[2] + p_ref[3])
    g_ref[...] = jnp.zeros(g_ref.shape, F32)
    gram = None
    for t in range(3):
        block = m_ref[t * HEAD : (t + 1) * HEAD, :]
        term = nt(block, block)
        gram = term if gram is None else gram + term
    g_ref[:128, :] = gram[:128, :128]
    g_ref[256:320, :64] = gram[128:, 128:]
    g_ref[320:384, :] = gram[128:, :128]
    block = m_ref[3 * HEAD : 704, :]
    g_ref[128:256, :] = nt(block, block)
    g_ref[384:392, :] = peak_ref[...]


def moment_and_gram(parts, peaks):
    return pl.pallas_call(
        gram_kernel,
        out_shape=(
            jax.ShapeDtypeStruct((704, 128), F32),
            jax.ShapeDtypeStruct((392, 128), F32),
        ),
        in_specs=[VMEM, VMEM],
        out_specs=(VMEM, VMEM),
        cost_estimate=pl.CostEstimate(flops=1000, bytes_accessed=1000, transcendentals=0),
        name="moment_and_gram",
    )(parts, peaks)


def full_dot(a, b):
    return jnp.dot(a, b, precision=FULL, preferred_element_type=F32)


def newton_factor(gram):
    size = gram.shape[0]
    eye = (
        lax.broadcasted_iota(jnp.int32, (size, size), 0)
        == lax.broadcasted_iota(jnp.int32, (size, size), 1)
    ).astype(F32)
    square = jnp.sum(jnp.sum(gram * eye, axis=1, keepdims=True), axis=0, keepdims=True)
    inverse = 1.0 / (jnp.sqrt(square) + 1e-07)
    a = gram * inverse * inverse
    product = None
    for step in range(NS_STEPS):
        factor = NS_A * eye + NS_B * a + NS_C * full_dot(a, a)
        product = factor if product is None else full_dot(product, factor)
        if step + 1 < NS_STEPS:
            a = full_dot(full_dot(factor, a), factor)
    return product * inverse


def newton_kernel(m_ref, a_ref, b_ref, c_ref, d_ref, *rest):
    out_ref = rest[-1]
    spot = (slice(384, 392), slice(0, 128))
    peaks = jnp.maximum(
        jnp.maximum(a_ref[spot], b_ref[spot]), jnp.maximum(c_ref[spot], d_ref[spot])
    )
    gram = (a_ref[...] + b_ref[...]) + (c_ref[...] + d_ref[...])
    low = gram[320:384, :]
    gram_q = jnp.concatenate(
        [
            jnp.concatenate([gram[:128, :], low.T], axis=1),
            jnp.concatenate([low, gram[256:320, :64]], axis=1),
        ],
        axis=0,
    )
    factor_q = newton_factor(gram_q) * (0.2 * math.sqrt(QR))
    factor_k = newton_factor(gram[128:256, :]) * (0.2 * math.sqrt(KVR))
    rows = []
    for t in range(3):
        block = m_ref[t * HEAD : (t + 1) * HEAD, :]
        rows.append(
            lax.dot_general(
                block, factor_q, (((0,), (0,)), ((), ())), precision=FULL, preferred_element_type=F32
            )
        )
    step = jnp.concatenate(rows, axis=0)
    step_k = lax.dot_general(
        m_ref[3 * HEAD : 704, :],
        factor_k,
        (((0,), (0,)), ((), ())),
        precision=FULL,
        preferred_element_type=F32,
    )
    out_ref[...] = jnp.zeros(out_ref.shape, F32)
    for i in range(8):
        out_ref[i, :48, :HEAD] = step[i * 48 : (i + 1) * 48, :]
        out_ref[i, 48:, :128] = step_k[i * 16 : (i + 1) * 16, :]
        out_ref[i, 48:56, 128:] = peaks


def newton(moment, grams, ties):
    return pl.pallas_call(
        newton_kernel,
        out_shape=jax.ShapeDtypeStruct((8, 64, 256), F32),
        in_specs=[VMEM] * 5 + [ANY] * len(ties),
        out_specs=VMEM,
        cost_estimate=pl.CostEstimate(flops=1000, bytes_accessed=1000, transcendentals=0),
        name="newton",
    )(moment, *grams, *ties)


def update_kernel(step_ref, wq_ref, wk_ref, flag_ref, sq_ref, sk_ref, nq_ref, nk_ref, peak_ref):
    peaks = step_ref[0, 48:56, 128:]
    for source in range(1, 8):
        peaks = jnp.maximum(peaks, step_ref[source, 48:56, 128:])
    peak_ref[...] = peaks
    ratio = CLIP_TAU / jnp.maximum(peaks, CLIP_TAU)
    gamma = jnp.concatenate(
        [jnp.where(flag_ref[h] > 0, ratio[h : h + 1], 1.0) for h in range(8)], axis=0
    )
    root = jnp.sqrt(gamma)
    keep = 1.0 - LEARN_RATE * DECAY
    lane = lax.broadcasted_iota(jnp.int32, (1, 384), 1)
    none = jnp.zeros((48, 128), F32)

    def source_of(head):
        return head % 4 * 2 + head // 4

    def thrice(row):
        return jnp.concatenate([row] * 3, axis=1)

    for pair in range(4):
        even, odd = 2 * pair, 2 * pair + 1
        step = jnp.concatenate([step_ref[source_of(even), :48, :], none], axis=1) + pltpu.roll(
            jnp.concatenate([step_ref[source_of(odd), :48, :], none], axis=1), HEAD, 1
        )
        columns = slice(pair * 384, (pair + 1) * 384)
        sq_ref[:, columns] = step
        factor = jnp.where(
            lane < HEAD,
            jnp.where(lane < NOPE, thrice(root[even : even + 1]), thrice(gamma[even : even + 1])),
            jnp.where(
                lane < HEAD + NOPE, thrice(root[odd : odd + 1]), thrice(gamma[odd : odd + 1])
            ),
        )
        nq_ref[:, columns] = (wq_ref[:, columns].astype(F32) * keep - LEARN_RATE * step) * factor
    for head in range(8):
        columns = slice(head * 128, (head + 1) * 128)
        step = step_ref[source_of(head), 48:, :128]
        sk_ref[:, columns] = step
        nk_ref[:, columns] = (
            wk_ref[:, columns].astype(F32) * keep - LEARN_RATE * step
        ) * root[head : head + 1]


def update(steps, owned_query, owned_key, flags):
    shapes = ((48, QR), (16, 1024), (48, QR), (16, 1024), (8, 128))
    return pl.pallas_call(
        update_kernel,
        out_shape=tuple(jax.ShapeDtypeStruct(shape, F32) for shape in shapes),
        in_specs=[VMEM] * 3 + [SMEM],
        out_specs=tuple(VMEM for _ in shapes),
        cost_estimate=pl.CostEstimate(flops=1000, bytes_accessed=1000, transcendentals=0),
        name="update",
    )(steps, owned_query, owned_key, flags)


def turn_tables(positions):
    frequency = ROPE_THETA ** (-2.0 * jnp.arange(ROPE // 2, dtype=F32) / ROPE)
    angles = positions.astype(F32)[:, None] * frequency[None, :]
    cosine, sine = jnp.cos(angles), jnp.sin(angles)
    none = jnp.zeros_like(cosine)
    return (
        jnp.concatenate([cosine, cosine, none, none], axis=1),
        jnp.concatenate([-sine, none, none, none], axis=1),
        jnp.concatenate([none, sine, none, none], axis=1),
    )


def look_up(table, index):
    hit = index[:, None] == jnp.arange(table.shape[0], dtype=jnp.int32)[None, :]
    return jnp.sum(jnp.where(hit, table[None, :], 0), axis=1)


def shards(
    q_latent,
    kv_latent,
    key_rope,
    block_order,
    w_query,
    w_key,
    w_value,
    grad_query,
    grad_key,
    mom_query,
    mom_key,
    clip_flags,
):
    z, x, c = lax.axis_index("z"), lax.axis_index("x"), lax.axis_index("c")
    yl, yh = lax.axis_index("yl"), lax.axis_index("yh")
    ctx = z * 8 + x * 2 + yl
    rows_in = jnp.concatenate(
        [q_latent, kv_latent, key_rope, jnp.zeros((64, 64), BF16)], axis=1
    )
    key_rows = rows_in[:, QR:]
    flips = [rows_in] + [flip(rows_in, k) for k in (1, 2, 3)]
    swapped = [swap_core(piece) for piece in flips]

    def other_half(first, second):
        def pick(array):
            width = array.shape[1] // 2
            return jnp.where(yl == 0, array[:, width:], array[:, :width])

        return pick(first), pick(second)

    g_other = jnp.concatenate(other_half(grad_query, grad_key), axis=1)
    g_other = lax.ppermute(g_other, "yl", [(0, 1), (1, 0)])
    mom_q, mom_k = other_half(mom_query, mom_key)
    m_other = jnp.concatenate([mom_q, jnp.pad(mom_k, ((0, 0), (0, 256)))], axis=0)
    m_other = lax.ppermute(m_other, "yl", [(0, 1), (1, 0)])
    plane = lax.all_to_all(
        jnp.broadcast_to(key_rows[None], (16, 64, WIDE)), ("z", "x"), 0, 0
    )
    near = [flip(plane[:8], 1), flip(plane[:8], 3), flip(plane[8:], 1), flip(plane[8:], 3)]
    at = jnp.stack([c, z, x, yl, yh]).astype(jnp.int32)
    terms, l_own = gradient_terms(
        at, grad_query, grad_key, g_other, mom_query, mom_key, m_other, flips + swapped, []
    )
    terms = exchange(terms, FIRST)
    local_rows = jnp.arange(256, dtype=jnp.int32)
    qpos = look_up(block_order, 2 * ctx + jnp.arange(2, dtype=jnp.int32))
    query_pos = jnp.where(local_rows < 128, qpos[0], qpos[1]) * 128 + local_rows % 128
    wide = project_queries(l_own, w_query, w_key, *turn_tables(query_pos))
    far = [flip(near[1], 1), flip(near[2], 3)]
    mine = [plane, *near, *far]
    pieces = mine + [swap_core(piece) for piece in mine]
    slot = jnp.arange(16, dtype=jnp.int32)
    place = jnp.concatenate(
        [
            look_up(
                block_order,
                2 * (slot // 4 * 8 + slot % 4 * 2 + (yl ^ (k & 1))) + (yh ^ (k >> 1)),
            )
            for k in (0, 1, 3, 2)
        ]
    )
    place = jnp.concatenate([place[:24], place[32:40], place[24:32], place[40:]])
    core_rows = jnp.stack([c * 64, 64 - c * 64]).astype(jnp.int32)

    terms = sum_first(terms, [])
    parts = exchange(terms, SECOND)
    attn_out, peaks = attention(
        0, 8, place, core_rows, qpos, wide, w_value, pieces, [mark_after([*near, wide])]
    )
    moment, gram = moment_and_gram(parts, peaks)
    grams = [gram] + [move_z(gram, k) for k in (1, 2, 3)]
    steps = newton(moment, grams, [])
    steps = lax.all_to_all(steps, ("x", "yl"), 0, 0)
    step_query, step_key, new_query, new_key, head_peaks = update(
        steps,
        lax.dynamic_slice_in_dim(w_query, ctx * 48, 48, 0),
        lax.dynamic_slice_in_dim(w_key, ctx * 16, 16, 0),
        clip_flags,
    )
    return (attn_out, head_peaks[:, 0], step_query, step_key, new_query, new_key)


def solution(mesh):
    fine = Mesh(mesh.devices.reshape(4, 4, 2, 2, 2), ("z", "x", "yl", "yh", "c"))
    ctx, dp = ("z", "x", "yl"), ("yh", "c")
    tokens = P(ctx + dp, None)
    columns = P(None, dp)
    both = P(ctx, dp)
    in_specs = (
        tokens,
        tokens,
        tokens,
        P(),
        columns,
        columns,
        columns,
        both,
        both,
        both,
        both,
        P(dp),
    )
    out_specs = (both, P(dp), both, both, both, both)
    return jax.shard_map(shards, mesh=fine, in_specs=in_specs, out_specs=out_specs, check_vma=False)
```

```python
import functools
import math

import jax
import jax.numpy as jnp
from jax import lax
from jax.experimental import pallas as pl
from jax.experimental.pallas import tpu as pltpu
from jax.sharding import Mesh
from jax.sharding import PartitionSpec as P

QR = 1536
KVR = 512
NOPE = 128
ROPE = 64
WIDE = 640
NS_STEPS = 3
NS_A = 3.4445
NS_B = -4.775
NS_C = 2.0315
MOMENTUM = 0.95
LEARN_RATE = 0.05
DECAY = 0.1
CLIP_TAU = 6.0
ROPE_THETA = 50000.0
HEAD = NOPE + ROPE
SCALE = HEAD ** (-0.5)
LOG2E = math.log2(math.e)
FULL = lax.Precision.HIGHEST
F32 = jnp.float32
BF16 = jnp.bfloat16
LOW = -1e30
ANY = pl.BlockSpec(memory_space=pl.ANY)
VMEM = pl.BlockSpec(memory_space=pltpu.VMEM)
SMEM = pl.BlockSpec(memory_space=pltpu.SMEM)
TILE = 512


def place_of(z, x, c):
    return (z * 4 + x) * 2 + c


FOUR = range(4)
ALONG_Z = [[[place_of(z, x, c) for z in FOUR] for x in FOUR] for c in range(2)]
ALONG_X = [[[place_of(z, x, c) for x in FOUR] for z in FOUR] for c in range(2)]
FIRST = ALONG_Z[0] + ALONG_X[1]
SECOND = ALONG_X[0] + ALONG_Z[1]


def exchange(value, groups):
    return lax.all_to_all(value, ("z", "x", "c"), 0, 0, axis_index_groups=groups)


def move_z(value, k):
    return lax.ppermute(value, "z", [(i, (i + k) % 4) for i in range(4)])


def flip(value, k):
    pairs = []
    for yl in range(2):
        for yh in range(2):
            pairs.append((yl * 2 + yh, (yl ^ (k & 1)) * 2 + (yh ^ (k >> 1))))
    return lax.ppermute(value, ("yl", "yh"), pairs)


def swap_core(value):
    return lax.ppermute(value, "c", [(0, 1), (1, 0)])


def attention_kernel(head0, heads, count, *refs):
    place_ref, core_ref, qpos_ref, q_ref, wv_ref = refs[:5]
    pieces = refs[5 : 5 + count]
    out_ref, peak_ref, acc, top, total, keys, sem = refs[-7:]
    width = heads * 128
    slot = 0
    for index, piece in enumerate(pieces):
        side = 0 if index < count // 2 else 1
        if index == count // 2:
            slot = 0

        @pl.loop(0, piece.shape[0])
        def _(s, piece=piece, side=side, slot=slot):
            row = pl.multiple_of(place_ref[slot + s] * 128 + core_ref[side], 64)
            pltpu.make_async_copy(piece.at[s], keys.at[pl.ds(row, 64)], sem).start()

        slot += piece.shape[0]
    pltpu.make_async_copy(keys, keys, sem).wait()
    factor = SCALE * LOG2E
    for half in range(2):
        acc[...] = jnp.zeros(acc.shape, F32)
        top[...] = jnp.full(top.shape, LOW, F32)
        total[...] = jnp.zeros(total.shape, F32)
        tiles = lax.div(qpos_ref[half] + 4, 4)

        def tile(j, masked, half=half):
            row0 = pl.multiple_of(j * TILE, TILE)
            k = keys[pl.ds(row0, TILE), :]
            s = lax.dot_general(
                q_ref[half, head0 * 128 : head0 * 128 + width, :],
                k,
                (((1,), (1,)), ((), ())),
                preferred_element_type=F32,
            )
            s = [s[:, b * 128 : (b + 1) * 128] for b in range(4)]
            if masked:
                row_pos = qpos_ref[half] * 128 + (
                    lax.broadcasted_iota(jnp.int32, (width, 128), 0) & 127
                )
                col = lax.broadcasted_iota(jnp.int32, (width, 128), 1)
                s = [
                    jnp.where((j * 4 + b) * 128 + col <= row_pos, s[b], LOW) for b in range(4)
                ]
            old = top[...]
            peak = jnp.maximum(jnp.maximum(s[0], s[1]), jnp.maximum(s[2], s[3]))
            new = jnp.maximum(old, jnp.max(peak, axis=1, keepdims=True))
            p = [jnp.exp2((part - new) * factor) for part in s]
            keep = jnp.exp2((old - new) * factor)
            top[...] = new
            total[...] = total[...] * keep + ((p[0] + p[1]) + (p[2] + p[3]))
            weights = jnp.concatenate(p, axis=1).astype(BF16)
            acc[...] = acc[...] * jnp.concatenate([keep] * 4, axis=1) + jnp.dot(
                weights, k[:, :KVR], preferred_element_type=F32
            )

        @pl.loop(0, tiles - 1)
        def _(j):
            tile(j, False)

        tile(tiles - 1, True)
        for h in range(heads):
            rows = pl.ds(h * 128, 128)
            latent = acc[rows, :] / jnp.sum(total[rows, :], axis=1, keepdims=True)
            first = (head0 + h) * 128
            o = jnp.dot(
                latent.astype(BF16), wv_ref[:, first : first + 128], preferred_element_type=F32
            )
            out_ref[half * 128 : (half + 1) * 128, h * 128 : (h + 1) * 128] = (
                o * KVR ** (-0.5)
            ).astype(BF16)
            peak = jnp.max(top[rows, :], axis=0, keepdims=True) * SCALE
            if half == 0:
                peak_ref[h : h + 1, :] = peak
            else:
                peak_ref[h : h + 1, :] = jnp.maximum(peak_ref[h : h + 1, :], peak)


def attention(head0, heads, place, core_rows, qpos, queries, w_value, pieces, ties):
    width = heads * 128
    return pl.pallas_call(
        functools.partial(attention_kernel, head0, heads, len(pieces)),
        out_shape=(
            jax.ShapeDtypeStruct((256, width), BF16),
            jax.ShapeDtypeStruct((heads, 128), F32),
        ),
        in_specs=[SMEM] * 3 + [VMEM] * 2 + [ANY] * (len(pieces) + len(ties)),
        out_specs=(VMEM, VMEM),
        scratch_shapes=[
            pltpu.VMEM((width, KVR), F32),
            pltpu.VMEM((width, 128), F32),
            pltpu.VMEM((width, 128), F32),
            pltpu.VMEM((8192, WIDE), BF16),
            pltpu.SemaphoreType.DMA,
        ],
        compiler_params=pltpu.CompilerParams(vmem_limit_bytes=52 * 2**20),
        cost_estimate=pl.CostEstimate(
            flops=20 * heads // 8 * 10**9,
            bytes_accessed=14 * 2**20,
            transcendentals=heads * 10**6,
        ),
        name="attention",
    )(place, core_rows, qpos, queries, w_value, *pieces, *ties)


def mark_kernel(*refs):
    refs[-1][...] = jnp.zeros((8, 128), F32)


def mark_after(ties):
    return pl.pallas_call(
        mark_kernel,
        out_shape=jax.ShapeDtypeStruct((8, 128), F32),
        in_specs=[ANY] * len(ties),
        out_specs=VMEM,
        compiler_params=pltpu.CompilerParams(vmem_limit_bytes=2**20),
        cost_estimate=pl.CostEstimate(flops=34 * 10**9, bytes_accessed=1000, transcendentals=0),
        name="mark",
    )(*ties)


def query_kernel(l_ref, wq_ref, wk_ref, cos_ref, low_ref, high_ref, out_ref):
    for pair in range(4):
        both = (
            jnp.dot(
                l_ref[:, :QR],
                wq_ref[:, pair * 384 : (pair + 1) * 384],
                preferred_element_type=F32,
            )
            * QR ** (-0.5)
        )
        for odd in range(2):
            q = pltpu.roll(both, HEAD, 1) if odd else both
            h = 2 * pair + odd
            nope = q[:, :NOPE].astype(BF16)
            turn = q[:, NOPE : 2 * NOPE]
            turned = (
                turn * cos_ref[...]
                + pltpu.roll(turn, 96, 1) * low_ref[...]
                + pltpu.roll(turn, 32, 1) * high_ref[...]
            ).astype(BF16)
            absorbed = (
                lax.dot_general(
                    nope,
                    wk_ref[:, h * NOPE : (h + 1) * NOPE],
                    (((1,), (1,)), ((), ())),
                    preferred_element_type=F32,
                )
                * KVR ** (-0.5)
            ).astype(BF16)
            for half in range(2):
                rows = slice(half * 128, (half + 1) * 128)
                out_ref[half, h * 128 : (h + 1) * 128, :KVR] = absorbed[rows]
                out_ref[half, h * 128 : (h + 1) * 128, KVR:] = turned[rows]


def project_queries(l_own, w_query, w_key, cosine, low, high):
    return pl.pallas_call(
        query_kernel,
        out_shape=jax.ShapeDtypeStruct((2, 1024, WIDE), BF16),
        in_specs=[VMEM] * 6,
        out_specs=VMEM,
        compiler_params=pltpu.CompilerParams(vmem_limit_bytes=32 * 2**20),
        cost_estimate=pl.CostEstimate(flops=1000, bytes_accessed=1000, transcendentals=0),
        name="queries",
    )(l_own, w_query, w_key, cosine, low, high)


def gradient_kernel(at_ref, gq_ref, gk_ref, g_other, mq_ref, mk_ref, m_other, *rest):
    shards_own, shards_swapped = rest[:4], rest[4:8]
    out_ref, l_own, l_other, gq_t, gk_t, mq_t, mk_t = rest[-7:]
    core, z, x, yl, yh = (at_ref[i] for i in range(5))
    for k in range(4):
        target = l_other if k & 1 else l_own
        block = jnp.bitwise_xor(yh, k >> 1) * 128
        for side, shard in ((core, shards_own[k]), (1 - core, shards_swapped[k])):
            target[pl.ds(pl.multiple_of(block + side * 64, 64), 64), :] = shard[...]
    wide_q = pl.ds(pl.multiple_of(yl * 768, 128), 768)
    wide_k = pl.ds(pl.multiple_of(yl * 512, 128), 512)
    gq_t[0] = gq_ref[:, wide_q].T
    gk_t[0] = gk_ref[:, wide_k].T
    gq_t[1] = g_other[:, :768].T
    gk_t[1] = g_other[:, 768:].T

    def spread(own, other):
        low = jnp.where(yl == 0, own, other)
        high = jnp.where(yl == 0, other, own)
        pair = jnp.concatenate([low, high], axis=0)
        rows = [jnp.where(x == i, MOMENTUM, 0.0) * pair for i in range(4)]
        return jnp.concatenate(rows, axis=0).T

    mq_t[...] = spread(mq_ref[:, wide_q], m_other[:48, :])
    mk_t[...] = spread(mk_ref[:, wide_k], m_other[48:, :512])
    for zb in range(4):
        mine = jnp.where(z == zb, 1.0, 0.0)

        def block(g, cols):
            return jnp.dot(g[0], l_own[:, cols], preferred_element_type=F32) + jnp.dot(
                g[1], l_other[:, cols], preferred_element_type=F32
            )

        m = block(gq_t, slice(zb * 384, (zb + 1) * 384)) + mine * mq_t[...]
        mk = block(gk_t, slice(QR + zb * 128, QR + (zb + 1) * 128)) + mine * mk_t[...]
        for xb in range(4):
            k = jnp.where(core == 0, zb, xb)
            j = jnp.where(core == 0, xb, zb)
            for t in range(3):
                out_ref[k, j, t * HEAD : (t + 1) * HEAD, :] = m[
                    xb * HEAD : (xb + 1) * HEAD, t * 128 : (t + 1) * 128
                ]
            out_ref[k, j, 3 * HEAD : 704, :] = mk[xb * 128 : (xb + 1) * 128, :]


def gradient_terms(at, grad_query, grad_key, g_other, mom_query, mom_key, m_other, shards, ties):
    return pl.pallas_call(
        gradient_kernel,
        out_shape=(
            jax.ShapeDtypeStruct((4, 4, 704, 128), F32),
            jax.ShapeDtypeStruct((256, QR + WIDE), BF16),
        ),
        in_specs=[SMEM] + [VMEM] * 14 + [ANY] * len(ties),
        out_specs=(VMEM, VMEM),
        scratch_shapes=[
            pltpu.VMEM((256, QR + WIDE), BF16),
            pltpu.VMEM((2, 768, 256), BF16),
            pltpu.VMEM((2, 512, 256), BF16),
            pltpu.VMEM((768, 384), F32),
            pltpu.VMEM((512, 128), F32),
        ],
        compiler_params=pltpu.CompilerParams(vmem_limit_bytes=56 * 2**20),
        cost_estimate=pl.CostEstimate(flops=1000, bytes_accessed=1000, transcendentals=0),
        name="gradient_terms",
    )(at, grad_query, grad_key, g_other, mom_query, mom_key, m_other, *shards, *ties)


def sum_kernel(a_ref, *rest):
    rest[-1][0] = (a_ref[0, 0] + a_ref[1, 0]) + (a_ref[2, 0] + a_ref[3, 0])


def sum_first(terms, ties):
    return pl.pallas_call(
        sum_kernel,
        grid=(4,),
        out_shape=jax.ShapeDtypeStruct((4, 704, 128), F32),
        in_specs=[pl.BlockSpec((4, 1, 704, 128), lambda j: (0, j, 0, 0))] + [ANY] * len(ties),
        out_specs=pl.BlockSpec((1, 704, 128), lambda j: (j, 0, 0)),
        compiler_params=pltpu.CompilerParams(vmem_limit_bytes=16 * 2**20),
        cost_estimate=pl.CostEstimate(flops=1000, bytes_accessed=1000, transcendentals=0),
        name="sum_first",
    )(terms, *ties)


def nt(a, b):
    return lax.dot_general(
        a, b, (((1,), (1,)), ((), ())), precision=FULL, preferred_element_type=F32
    )


def gram_kernel(p_ref, peak_ref, m_ref, g_ref):
    m_ref[...] = (p_ref[0] + p_ref[1]) + (p_ref[2] + p_ref[3])
    g_ref[...] = jnp.zeros(g_ref.shape, F32)
    gram = None
    for t in range(3):
        block = m_ref[t * HEAD : (t + 1) * HEAD, :]
        term = nt(block, block)
        gram = term if gram is None else gram + term
    g_ref[:128, :] = gram[:128, :128]
    g_ref[256:320, :64] = gram[128:, 128:]
    g_ref[320:384, :] = gram[128:, :128]
    block = m_ref[3 * HEAD : 704, :]
    g_ref[128:256, :] = nt(block, block)
    g_ref[384:392, :] = peak_ref[...]


def moment_and_gram(parts, peaks):
    return pl.pallas_call(
        gram_kernel,
        out_shape=(
            jax.ShapeDtypeStruct((704, 128), F32),
            jax.ShapeDtypeStruct((392, 128), F32),
        ),
        in_specs=[VMEM, VMEM],
        out_specs=(VMEM, VMEM),
        compiler_params=pltpu.CompilerParams(vmem_limit_bytes=16 * 2**20),
        cost_estimate=pl.CostEstimate(flops=1000, bytes_accessed=1000, transcendentals=0),
        name="moment_and_gram",
    )(parts, peaks)


def full_dot(a, b):
    return jnp.dot(a, b, precision=FULL, preferred_element_type=F32)


def newton_factors(grams):
    eyes, inverses, a = [], [], []
    for gram in grams:
        size = gram.shape[0]
        eye = (
            lax.broadcasted_iota(jnp.int32, (size, size), 0)
            == lax.broadcasted_iota(jnp.int32, (size, size), 1)
        ).astype(F32)
        square = jnp.sum(jnp.sum(gram * eye, axis=1, keepdims=True), axis=0, keepdims=True)
        inverse = 1.0 / (jnp.sqrt(square) + 1e-07)
        eyes.append(eye)
        inverses.append(inverse)
        a.append(gram * inverse * inverse)
    pairs = range(len(grams))
    products = None
    for step in range(NS_STEPS):
        squares = [full_dot(a[i], a[i]) for i in pairs]
        factors = [NS_A * eyes[i] + NS_B * a[i] + NS_C * squares[i] for i in pairs]
        if step + 1 < NS_STEPS:
            halfway = [full_dot(factors[i], a[i]) for i in pairs]
            a = [full_dot(halfway[i], factors[i]) for i in pairs]
        if products is None:
            products = factors
        else:
            products = [full_dot(products[i], factors[i]) for i in pairs]
    return [products[i] * inverses[i] for i in pairs]


def newton_kernel(m_ref, a_ref, b_ref, c_ref, d_ref, *rest):
    out_ref = rest[-1]
    spot = (slice(384, 392), slice(0, 128))
    peaks = jnp.maximum(
        jnp.maximum(a_ref[spot], b_ref[spot]), jnp.maximum(c_ref[spot], d_ref[spot])
    )
    gram = (a_ref[...] + b_ref[...]) + (c_ref[...] + d_ref[...])
    low = gram[320:384, :]
    gram_q = jnp.concatenate(
        [
            jnp.concatenate([gram[:128, :], low.T], axis=1),
            jnp.concatenate([low, gram[256:320, :64]], axis=1),
        ],
        axis=0,
    )
    factor_q, factor_k = newton_factors([gram_q, gram[128:256, :]])
    factor_q = factor_q * (0.2 * math.sqrt(QR))
    factor_k = factor_k * (0.2 * math.sqrt(KVR))
    rows = []
    for t in range(3):
        block = m_ref[t * HEAD : (t + 1) * HEAD, :]
        rows.append(
            lax.dot_general(
                block, factor_q, (((0,), (0,)), ((), ())), precision=FULL, preferred_element_type=F32
            )
        )
    step = jnp.concatenate(rows, axis=0)
    step_k = lax.dot_general(
        m_ref[3 * HEAD : 704, :],
        factor_k,
        (((0,), (0,)), ((), ())),
        precision=FULL,
        preferred_element_type=F32,
    )
    out_ref[...] = jnp.zeros(out_ref.shape, F32)
    for i in range(8):
        out_ref[i, :48, :HEAD] = step[i * 48 : (i + 1) * 48, :]
        out_ref[i, 48:, :128] = step_k[i * 16 : (i + 1) * 16, :]
        out_ref[i, 48:56, 128:] = peaks


def newton(moment, grams, ties):
    return pl.pallas_call(
        newton_kernel,
        out_shape=jax.ShapeDtypeStruct((8, 64, 256), F32),
        in_specs=[VMEM] * 5 + [ANY] * len(ties),
        out_specs=VMEM,
        compiler_params=pltpu.CompilerParams(vmem_limit_bytes=16 * 2**20),
        cost_estimate=pl.CostEstimate(flops=1000, bytes_accessed=1000, transcendentals=0),
        name="newton",
    )(moment, *grams, *ties)


def update_kernel(step_ref, wq_ref, wk_ref, flag_ref, sq_ref, sk_ref, nq_ref, nk_ref, peak_ref):
    peaks = step_ref[0, 48:56, 128:]
    for source in range(1, 8):
        peaks = jnp.maximum(peaks, step_ref[source, 48:56, 128:])
    on_diagonal = lax.broadcasted_iota(jnp.int32, (8, 128), 0) == lax.broadcasted_iota(
        jnp.int32, (8, 128), 1
    )
    peak_ref[...] = jnp.sum(jnp.where(on_diagonal, peaks, 0.0), axis=0, keepdims=True)[:, :8]
    ratio = CLIP_TAU / jnp.maximum(peaks, CLIP_TAU)
    gamma = jnp.concatenate(
        [jnp.where(flag_ref[h] > 0, ratio[h : h + 1], 1.0) for h in range(8)], axis=0
    )
    root = jnp.sqrt(gamma)
    keep = 1.0 - LEARN_RATE * DECAY
    lane = lax.broadcasted_iota(jnp.int32, (1, 384), 1)
    none = jnp.zeros((48, 128), F32)

    def source_of(head):
        return head % 4 * 2 + head // 4

    def thrice(row):
        return jnp.concatenate([row] * 3, axis=1)

    for pair in range(4):
        even, odd = 2 * pair, 2 * pair + 1
        step = jnp.concatenate([step_ref[source_of(even), :48, :], none], axis=1) + pltpu.roll(
            jnp.concatenate([step_ref[source_of(odd), :48, :], none], axis=1), HEAD, 1
        )
        columns = slice(pair * 384, (pair + 1) * 384)
        sq_ref[:, columns] = step
        factor = jnp.where(
            lane < HEAD,
            jnp.where(lane < NOPE, thrice(root[even : even + 1]), thrice(gamma[even : even + 1])),
            jnp.where(
                lane < HEAD + NOPE, thrice(root[odd : odd + 1]), thrice(gamma[odd : odd + 1])
            ),
        )
        nq_ref[:, columns] = (wq_ref[:, columns].astype(F32) * keep - LEARN_RATE * step) * factor
    for head in range(8):
        columns = slice(head * 128, (head + 1) * 128)
        step = step_ref[source_of(head), 48:, :128]
        sk_ref[:, columns] = step
        nk_ref[:, columns] = (
            wk_ref[:, columns].astype(F32) * keep - LEARN_RATE * step
        ) * root[head : head + 1]


def update(steps, owned_query, owned_key, flags):
    shapes = ((48, QR), (16, 1024), (48, QR), (16, 1024), (1, 8))
    return pl.pallas_call(
        update_kernel,
        out_shape=tuple(jax.ShapeDtypeStruct(shape, F32) for shape in shapes),
        in_specs=[VMEM] * 3 + [SMEM],
        out_specs=tuple(VMEM for _ in shapes),
        compiler_params=pltpu.CompilerParams(vmem_limit_bytes=16 * 2**20),
        cost_estimate=pl.CostEstimate(flops=1000, bytes_accessed=1000, transcendentals=0),
        name="update",
    )(steps, owned_query, owned_key, flags)


def turn_tables(positions):
    frequency = ROPE_THETA ** (-2.0 * jnp.arange(ROPE // 2, dtype=F32) / ROPE)
    angles = positions.astype(F32)[:, None] * frequency[None, :]
    cosine, sine = jnp.cos(angles), jnp.sin(angles)
    none = jnp.zeros_like(cosine)
    return (
        jnp.concatenate([cosine, cosine, none, none], axis=1),
        jnp.concatenate([-sine, none, none, none], axis=1),
        jnp.concatenate([none, sine, none, none], axis=1),
    )


def look_up(table, index):
    hit = index[:, None] == jnp.arange(table.shape[0], dtype=jnp.int32)[None, :]
    return jnp.sum(jnp.where(hit, table[None, :], 0), axis=1)


def shards(
    q_latent,
    kv_latent,
    key_rope,
    block_order,
    w_query,
    w_key,
    w_value,
    grad_query,
    grad_key,
    mom_query,
    mom_key,
    clip_flags,
):
    z, x, c = lax.axis_index("z"), lax.axis_index("x"), lax.axis_index("c")
    yl, yh = lax.axis_index("yl"), lax.axis_index("yh")
    ctx = z * 8 + x * 2 + yl
    rows_in = jnp.concatenate(
        [q_latent, kv_latent, key_rope, jnp.zeros((64, 64), BF16)], axis=1
    )
    key_rows = rows_in[:, QR:]
    flips = [rows_in] + [flip(rows_in, k) for k in (1, 2, 3)]
    swapped = [swap_core(piece) for piece in flips]

    def other_half(first, second):
        def pick(array):
            width = array.shape[1] // 2
            return jnp.where(yl == 0, array[:, width:], array[:, :width])

        return pick(first), pick(second)

    g_other = jnp.concatenate(other_half(grad_query, grad_key), axis=1)
    g_other = lax.ppermute(g_other, "yl", [(0, 1), (1, 0)])
    mom_q, mom_k = other_half(mom_query, mom_key)
    m_other = jnp.concatenate([mom_q, jnp.pad(mom_k, ((0, 0), (0, 256)))], axis=0)
    m_other = lax.ppermute(m_other, "yl", [(0, 1), (1, 0)])
    plane = lax.all_to_all(
        jnp.broadcast_to(key_rows[None], (16, 64, WIDE)), ("z", "x"), 0, 0
    )
    near = [flip(plane[:8], 1), flip(plane[:8], 3), flip(plane[8:], 1), flip(plane[8:], 3)]
    at = jnp.stack([c, z, x, yl, yh]).astype(jnp.int32)
    terms, l_own = gradient_terms(
        at, grad_query, grad_key, g_other, mom_query, mom_key, m_other, flips + swapped, []
    )
    terms = exchange(terms, FIRST)
    local_rows = jnp.arange(256, dtype=jnp.int32)
    qpos = look_up(block_order, 2 * ctx + jnp.arange(2, dtype=jnp.int32))
    query_pos = jnp.where(local_rows < 128, qpos[0], qpos[1]) * 128 + local_rows % 128
    wide = project_queries(l_own, w_query, w_key, *turn_tables(query_pos))
    far = [flip(near[1], 1), flip(near[2], 3)]
    mine = [plane, *near, *far]
    pieces = mine + [swap_core(piece) for piece in mine]
    slot = jnp.arange(16, dtype=jnp.int32)
    place = jnp.concatenate(
        [
            look_up(
                block_order,
                2 * (slot // 4 * 8 + slot % 4 * 2 + (yl ^ (k & 1))) + (yh ^ (k >> 1)),
            )
            for k in (0, 1, 3, 2)
        ]
    )
    place = jnp.concatenate([place[:24], place[32:40], place[24:32], place[40:]])
    core_rows = jnp.stack([c * 64, 64 - c * 64]).astype(jnp.int32)

    terms = sum_first(terms, [])
    parts = exchange(terms, SECOND)
    attn_out, peaks = attention(
        0, 8, place, core_rows, qpos, wide, w_value, pieces, [mark_after([*near, wide])]
    )
    moment, gram = moment_and_gram(parts, peaks)
    grams = [gram] + [move_z(gram, k) for k in (1, 2, 3)]
    steps = newton(moment, grams, [])
    steps = lax.all_to_all(steps, ("x", "yl"), 0, 0)
    step_query, step_key, new_query, new_key, head_peaks = update(
        steps,
        lax.dynamic_slice_in_dim(w_query, ctx * 48, 48, 0),
        lax.dynamic_slice_in_dim(w_key, ctx * 16, 16, 0),
        clip_flags,
    )
    return (attn_out, head_peaks.reshape(8), step_query, step_key, new_query, new_key)


def solution(mesh):
    fine = Mesh(mesh.devices.reshape(4, 4, 2, 2, 2), ("z", "x", "yl", "yh", "c"))
    ctx, dp = ("z", "x", "yl"), ("yh", "c")
    tokens = P(ctx + dp, None)
    columns = P(None, dp)
    both = P(ctx, dp)
    in_specs = (
        tokens,
        tokens,
        tokens,
        P(),
        columns,
        columns,
        columns,
        both,
        both,
        both,
        both,
        P(dp),
    )
    out_specs = (both, P(dp), both, both, both, both)
    return jax.shard_map(shards, mesh=fine, in_specs=in_specs, out_specs=out_specs, check_vma=False)
```

```python
import functools
import math

import jax
import jax.numpy as jnp
from jax import lax
from jax.experimental import pallas as pl
from jax.experimental.pallas import tpu as pltpu
from jax.sharding import Mesh
from jax.sharding import PartitionSpec as P

QR = 1536
KVR = 512
NOPE = 128
ROPE = 64
WIDE = 640
NS_STEPS = 3
NS_A = 3.4445
NS_B = -4.775
NS_C = 2.0315
MOMENTUM = 0.95
LEARN_RATE = 0.05
DECAY = 0.1
CLIP_TAU = 6.0
ROPE_THETA = 50000.0
HEAD = NOPE + ROPE
SCALE = HEAD ** (-0.5)
LOG2E = math.log2(math.e)
FULL = lax.Precision.HIGHEST
F32 = jnp.float32
BF16 = jnp.bfloat16
LOW = -1e30
ANY = pl.BlockSpec(memory_space=pl.ANY)
VMEM = pl.BlockSpec(memory_space=pltpu.VMEM)
SMEM = pl.BlockSpec(memory_space=pltpu.SMEM)
TILE = 512


def place_of(z, x, c):
    return (z * 4 + x) * 2 + c


FOUR = range(4)
ALONG_Z = [[[place_of(z, x, c) for z in FOUR] for x in FOUR] for c in range(2)]
ALONG_X = [[[place_of(z, x, c) for x in FOUR] for z in FOUR] for c in range(2)]
FIRST = ALONG_Z[0] + ALONG_X[1]
SECOND = ALONG_X[0] + ALONG_Z[1]


def exchange(value, groups):
    return lax.all_to_all(value, ("z", "x", "c"), 0, 0, axis_index_groups=groups)


def move_z(value, k):
    return lax.ppermute(value, "z", [(i, (i + k) % 4) for i in range(4)])


def flip(value, k):
    pairs = []
    for yl in range(2):
        for yh in range(2):
            pairs.append((yl * 2 + yh, (yl ^ (k & 1)) * 2 + (yh ^ (k >> 1))))
    return lax.ppermute(value, ("yl", "yh"), pairs)


def swap_core(value):
    return lax.ppermute(value, "c", [(0, 1), (1, 0)])


def attention_kernel(head0, heads, count, *refs):
    place_ref, core_ref, qpos_ref, q_ref, wv_ref = refs[:5]
    pieces = refs[5 : 5 + count]
    out_ref, peak_ref, acc, top, total, keys, sem = refs[-7:]
    width = heads * 128
    slot = 0
    for index, piece in enumerate(pieces):
        side = 0 if index < count // 2 else 1
        if index == count // 2:
            slot = 0

        @pl.loop(0, piece.shape[0], unroll=True)
        def _(s, piece=piece, side=side, slot=slot):
            row = pl.multiple_of(place_ref[slot + s] * 128 + core_ref[side], 64)
            pltpu.make_async_copy(piece.at[s], keys.at[pl.ds(row, 64)], sem).start()

        slot += piece.shape[0]
    factor = SCALE * LOG2E
    for half in range(2):
        acc[...] = jnp.zeros(acc.shape, F32)
        top[...] = jnp.full(top.shape, LOW, F32)
        total[...] = jnp.zeros(total.shape, F32)
        tiles = lax.div(qpos_ref[half] + 4, 4)
        if half == 0:
            pltpu.make_async_copy(keys, keys, sem).wait()

        def tile(j, masked, half=half):
            row0 = pl.multiple_of(j * TILE, TILE)
            k = keys[pl.ds(row0, TILE), :]
            s = lax.dot_general(
                q_ref[half, head0 * 128 : head0 * 128 + width, :],
                k,
                (((1,), (1,)), ((), ())),
                preferred_element_type=F32,
            )
            s = [s[:, b * 128 : (b + 1) * 128] for b in range(4)]
            if masked:
                row_pos = qpos_ref[half] * 128 + (
                    lax.broadcasted_iota(jnp.int32, (width, 128), 0) & 127
                )
                col = lax.broadcasted_iota(jnp.int32, (width, 128), 1)
                s = [
                    jnp.where((j * 4 + b) * 128 + col <= row_pos, s[b], LOW) for b in range(4)
                ]
            old = top[...]
            peak = jnp.maximum(jnp.maximum(s[0], s[1]), jnp.maximum(s[2], s[3]))
            new = jnp.maximum(old, jnp.max(peak, axis=1, keepdims=True))
            p = [jnp.exp2((part - new) * factor) for part in s]
            keep = jnp.exp2((old - new) * factor)
            top[...] = new
            total[...] = total[...] * keep + ((p[0] + p[1]) + (p[2] + p[3]))
            weights = jnp.concatenate(p, axis=1).astype(BF16)
            acc[...] = acc[...] * jnp.concatenate([keep] * 4, axis=1) + jnp.dot(
                weights, k[:, :KVR], preferred_element_type=F32
            )

        @pl.loop(0, tiles - 1)
        def _(j):
            tile(j, False)

        tile(tiles - 1, True)
        for h in range(heads):
            rows = pl.ds(h * 128, 128)
            latent = acc[rows, :] / jnp.sum(total[rows, :], axis=1, keepdims=True)
            first = (head0 + h) * 128
            o = jnp.dot(
                latent.astype(BF16), wv_ref[:, first : first + 128], preferred_element_type=F32
            )
            out_ref[half * 128 : (half + 1) * 128, h * 128 : (h + 1) * 128] = (
                o * KVR ** (-0.5)
            ).astype(BF16)
            peak = jnp.max(top[rows, :], axis=0, keepdims=True) * SCALE
            if half == 0:
                peak_ref[h : h + 1, :] = peak
            else:
                peak_ref[h : h + 1, :] = jnp.maximum(peak_ref[h : h + 1, :], peak)


def attention(head0, heads, place, core_rows, qpos, queries, w_value, pieces, ties):
    width = heads * 128
    return pl.pallas_call(
        functools.partial(attention_kernel, head0, heads, len(pieces)),
        out_shape=(
            jax.ShapeDtypeStruct((256, width), BF16),
            jax.ShapeDtypeStruct((heads, 128), F32),
        ),
        in_specs=[SMEM] * 3 + [VMEM] * 2 + [ANY] * (len(pieces) + len(ties)),
        out_specs=(VMEM, VMEM),
        scratch_shapes=[
            pltpu.VMEM((width, KVR), F32),
            pltpu.VMEM((width, 128), F32),
            pltpu.VMEM((width, 128), F32),
            pltpu.VMEM((8192, WIDE), BF16),
            pltpu.SemaphoreType.DMA,
        ],
        compiler_params=pltpu.CompilerParams(vmem_limit_bytes=52 * 2**20),
        cost_estimate=pl.CostEstimate(
            flops=20 * heads // 8 * 10**9,
            bytes_accessed=14 * 2**20,
            transcendentals=heads * 10**6,
        ),
        name="attention",
    )(place, core_rows, qpos, queries, w_value, *pieces, *ties)


def mark_kernel(*refs):
    refs[-1][...] = jnp.zeros((8, 128), F32)


def mark_after(ties):
    return pl.pallas_call(
        mark_kernel,
        out_shape=jax.ShapeDtypeStruct((8, 128), F32),
        in_specs=[ANY] * len(ties),
        out_specs=VMEM,
        compiler_params=pltpu.CompilerParams(vmem_limit_bytes=2**20),
        cost_estimate=pl.CostEstimate(flops=34 * 10**9, bytes_accessed=1000, transcendentals=0),
        name="mark",
    )(*ties)


def query_kernel(l_ref, wq_ref, wk_ref, cos_ref, low_ref, high_ref, out_ref):
    for pair in range(4):
        both = (
            jnp.dot(
                l_ref[:, :QR],
                wq_ref[:, pair * 384 : (pair + 1) * 384],
                preferred_element_type=F32,
            )
            * QR ** (-0.5)
        )
        for odd in range(2):
            q = pltpu.roll(both, HEAD, 1) if odd else both
            h = 2 * pair + odd
            nope = q[:, :NOPE].astype(BF16)
            turn = q[:, NOPE : 2 * NOPE]
            turned = (
                turn * cos_ref[...]
                + pltpu.roll(turn, 96, 1) * low_ref[...]
                + pltpu.roll(turn, 32, 1) * high_ref[...]
            ).astype(BF16)
            absorbed = (
                lax.dot_general(
                    nope,
                    wk_ref[:, h * NOPE : (h + 1) * NOPE],
                    (((1,), (1,)), ((), ())),
                    preferred_element_type=F32,
                )
                * KVR ** (-0.5)
            ).astype(BF16)
            for half in range(2):
                rows = slice(half * 128, (half + 1) * 128)
                out_ref[half, h * 128 : (h + 1) * 128, :KVR] = absorbed[rows]
                out_ref[half, h * 128 : (h + 1) * 128, KVR:] = turned[rows]


def project_queries(l_own, w_query, w_key, cosine, low, high):
    return pl.pallas_call(
        query_kernel,
        out_shape=jax.ShapeDtypeStruct((2, 1024, WIDE), BF16),
        in_specs=[VMEM] * 6,
        out_specs=VMEM,
        compiler_params=pltpu.CompilerParams(vmem_limit_bytes=32 * 2**20),
        cost_estimate=pl.CostEstimate(flops=1000, bytes_accessed=1000, transcendentals=0),
        name="queries",
    )(l_own, w_query, w_key, cosine, low, high)


def gradient_kernel(at_ref, gq_ref, gk_ref, g_other, mq_ref, mk_ref, m_other, *rest):
    shards_own, shards_swapped = rest[:4], rest[4:8]
    out_ref, l_own, l_other, gq_t, gk_t, mq_t, mk_t = rest[-7:]
    core, z, x, yl, yh = (at_ref[i] for i in range(5))
    for k in range(4):
        target = l_other if k & 1 else l_own
        block = jnp.bitwise_xor(yh, k >> 1) * 128
        for side, shard in ((core, shards_own[k]), (1 - core, shards_swapped[k])):
            target[pl.ds(pl.multiple_of(block + side * 64, 64), 64), :] = shard[...]
    wide_q = pl.ds(pl.multiple_of(yl * 768, 128), 768)
    wide_k = pl.ds(pl.multiple_of(yl * 512, 128), 512)
    gq_t[0] = gq_ref[:, wide_q].T
    gk_t[0] = gk_ref[:, wide_k].T
    gq_t[1] = g_other[:, :768].T
    gk_t[1] = g_other[:, 768:].T

    def spread(own, other):
        low = jnp.where(yl == 0, own, other)
        high = jnp.where(yl == 0, other, own)
        pair = jnp.concatenate([low, high], axis=0)
        rows = [jnp.where(x == i, MOMENTUM, 0.0) * pair for i in range(4)]
        return jnp.concatenate(rows, axis=0).T

    mq_t[...] = spread(mq_ref[:, wide_q], m_other[:48, :])
    mk_t[...] = spread(mk_ref[:, wide_k], m_other[48:, :512])
    for zb in range(4):
        mine = jnp.where(z == zb, 1.0, 0.0)

        def block(g, cols):
            return jnp.dot(g[0], l_own[:, cols], preferred_element_type=F32) + jnp.dot(
                g[1], l_other[:, cols], preferred_element_type=F32
            )

        m = block(gq_t, slice(zb * 384, (zb + 1) * 384)) + mine * mq_t[...]
        mk = block(gk_t, slice(QR + zb * 128, QR + (zb + 1) * 128)) + mine * mk_t[...]
        for xb in range(4):
            k = jnp.where(core == 0, zb, xb)
            j = jnp.where(core == 0, xb, zb)
            for t in range(3):
                out_ref[k, j, t * HEAD : (t + 1) * HEAD, :] = m[
                    xb * HEAD : (xb + 1) * HEAD, t * 128 : (t + 1) * 128
                ]
            out_ref[k, j, 3 * HEAD : 704, :] = mk[xb * 128 : (xb + 1) * 128, :]


def gradient_terms(at, grad_query, grad_key, g_other, mom_query, mom_key, m_other, shards, ties):
    return pl.pallas_call(
        gradient_kernel,
        out_shape=(
            jax.ShapeDtypeStruct((4, 4, 704, 128), F32),
            jax.ShapeDtypeStruct((256, QR + WIDE), BF16),
        ),
        in_specs=[SMEM] + [VMEM] * 14 + [ANY] * len(ties),
        out_specs=(VMEM, VMEM),
        scratch_shapes=[
            pltpu.VMEM((256, QR + WIDE), BF16),
            pltpu.VMEM((2, 768, 256), BF16),
            pltpu.VMEM((2, 512, 256), BF16),
            pltpu.VMEM((768, 384), F32),
            pltpu.VMEM((512, 128), F32),
        ],
        compiler_params=pltpu.CompilerParams(vmem_limit_bytes=56 * 2**20),
        cost_estimate=pl.CostEstimate(flops=1000, bytes_accessed=1000, transcendentals=0),
        name="gradient_terms",
    )(at, grad_query, grad_key, g_other, mom_query, mom_key, m_other, *shards, *ties)


def sum_kernel(a_ref, *rest):
    rest[-1][0] = (a_ref[0, 0] + a_ref[1, 0]) + (a_ref[2, 0] + a_ref[3, 0])


def sum_first(terms, ties):
    return pl.pallas_call(
        sum_kernel,
        grid=(4,),
        out_shape=jax.ShapeDtypeStruct((4, 704, 128), F32),
        in_specs=[pl.BlockSpec((4, 1, 704, 128), lambda j: (0, j, 0, 0))] + [ANY] * len(ties),
        out_specs=pl.BlockSpec((1, 704, 128), lambda j: (j, 0, 0)),
        compiler_params=pltpu.CompilerParams(vmem_limit_bytes=16 * 2**20),
        cost_estimate=pl.CostEstimate(flops=1000, bytes_accessed=1000, transcendentals=0),
        name="sum_first",
    )(terms, *ties)


def nt(a, b):
    return lax.dot_general(
        a, b, (((1,), (1,)), ((), ())), precision=FULL, preferred_element_type=F32
    )


def gram_kernel(p_ref, peak_ref, m_ref, g_ref):
    m_ref[...] = (p_ref[0] + p_ref[1]) + (p_ref[2] + p_ref[3])
    g_ref[...] = jnp.zeros(g_ref.shape, F32)
    gram = None
    for t in range(3):
        block = m_ref[t * HEAD : (t + 1) * HEAD, :]
        term = nt(block, block)
        gram = term if gram is None else gram + term
    g_ref[:128, :] = gram[:128, :128]
    g_ref[256:320, :64] = gram[128:, 128:]
    g_ref[320:384, :] = gram[128:, :128]
    block = m_ref[3 * HEAD : 704, :]
    g_ref[128:256, :] = nt(block, block)
    g_ref[384:392, :] = peak_ref[...]


def moment_and_gram(parts, peaks):
    return pl.pallas_call(
        gram_kernel,
        out_shape=(
            jax.ShapeDtypeStruct((704, 128), F32),
            jax.ShapeDtypeStruct((392, 128), F32),
        ),
        in_specs=[VMEM, VMEM],
        out_specs=(VMEM, VMEM),
        compiler_params=pltpu.CompilerParams(vmem_limit_bytes=16 * 2**20),
        cost_estimate=pl.CostEstimate(flops=1000, bytes_accessed=1000, transcendentals=0),
        name="moment_and_gram",
    )(parts, peaks)


def full_dot(a, b):
    return jnp.dot(a, b, precision=FULL, preferred_element_type=F32)


def newton_factors(grams):
    eyes, inverses, a = [], [], []
    for gram in grams:
        size = gram.shape[0]
        eye = (
            lax.broadcasted_iota(jnp.int32, (size, size), 0)
            == lax.broadcasted_iota(jnp.int32, (size, size), 1)
        ).astype(F32)
        square = jnp.sum(jnp.sum(gram * eye, axis=1, keepdims=True), axis=0, keepdims=True)
        inverse = 1.0 / (jnp.sqrt(square) + 1e-07)
        eyes.append(eye)
        inverses.append(inverse)
        a.append(gram * inverse * inverse)
    pairs = range(len(grams))
    products = None
    for step in range(NS_STEPS):
        squares = [full_dot(a[i], a[i]) for i in pairs]
        factors = [NS_A * eyes[i] + NS_B * a[i] + NS_C * squares[i] for i in pairs]
        if step + 1 < NS_STEPS:
            halfway = [full_dot(factors[i], a[i]) for i in pairs]
            a = [full_dot(halfway[i], factors[i]) for i in pairs]
        if products is None:
            products = factors
        else:
            products = [full_dot(products[i], factors[i]) for i in pairs]
    return [products[i] * inverses[i] for i in pairs]


def newton_kernel(m_ref, a_ref, b_ref, c_ref, d_ref, *rest):
    out_ref = rest[-1]
    spot = (slice(384, 392), slice(0, 128))
    peaks = jnp.maximum(
        jnp.maximum(a_ref[spot], b_ref[spot]), jnp.maximum(c_ref[spot], d_ref[spot])
    )
    gram = (a_ref[...] + b_ref[...]) + (c_ref[...] + d_ref[...])
    low = gram[320:384, :]
    gram_q = jnp.concatenate(
        [
            jnp.concatenate([gram[:128, :], low.T], axis=1),
            jnp.concatenate([low, gram[256:320, :64]], axis=1),
        ],
        axis=0,
    )
    factor_q, factor_k = newton_factors([gram_q, gram[128:256, :]])
    factor_q = factor_q * (0.2 * math.sqrt(QR))
    factor_k = factor_k * (0.2 * math.sqrt(KVR))
    rows = []
    for t in range(3):
        block = m_ref[t * HEAD : (t + 1) * HEAD, :]
        rows.append(
            lax.dot_general(
                block, factor_q, (((0,), (0,)), ((), ())), precision=FULL, preferred_element_type=F32
            )
        )
    step = jnp.concatenate(rows, axis=0)
    step_k = lax.dot_general(
        m_ref[3 * HEAD : 704, :],
        factor_k,
        (((0,), (0,)), ((), ())),
        precision=FULL,
        preferred_element_type=F32,
    )
    out_ref[...] = jnp.zeros(out_ref.shape, F32)
    for i in range(8):
        out_ref[i, :48, :HEAD] = step[i * 48 : (i + 1) * 48, :]
        out_ref[i, 48:, :128] = step_k[i * 16 : (i + 1) * 16, :]
        out_ref[i, 48:56, 128:] = peaks


def newton(moment, grams, ties):
    return pl.pallas_call(
        newton_kernel,
        out_shape=jax.ShapeDtypeStruct((8, 64, 256), F32),
        in_specs=[VMEM] * 5 + [ANY] * len(ties),
        out_specs=VMEM,
        compiler_params=pltpu.CompilerParams(vmem_limit_bytes=16 * 2**20),
        cost_estimate=pl.CostEstimate(flops=1000, bytes_accessed=1000, transcendentals=0),
        name="newton",
    )(moment, *grams, *ties)


def update_kernel(step_ref, wq_ref, wk_ref, flag_ref, sq_ref, sk_ref, nq_ref, nk_ref, peak_ref):
    peaks = step_ref[0, 48:56, 128:]
    for source in range(1, 8):
        peaks = jnp.maximum(peaks, step_ref[source, 48:56, 128:])
    on_diagonal = lax.broadcasted_iota(jnp.int32, (8, 128), 0) == lax.broadcasted_iota(
        jnp.int32, (8, 128), 1
    )
    peak_ref[...] = jnp.sum(jnp.where(on_diagonal, peaks, 0.0), axis=0, keepdims=True)[:, :8]
    ratio = CLIP_TAU / jnp.maximum(peaks, CLIP_TAU)
    gamma = jnp.concatenate(
        [jnp.where(flag_ref[h] > 0, ratio[h : h + 1], 1.0) for h in range(8)], axis=0
    )
    root = jnp.sqrt(gamma)
    keep = 1.0 - LEARN_RATE * DECAY
    lane = lax.broadcasted_iota(jnp.int32, (1, 384), 1)
    none = jnp.zeros((48, 128), F32)

    def source_of(head):
        return head % 4 * 2 + head // 4

    def thrice(row):
        return jnp.concatenate([row] * 3, axis=1)

    for pair in range(4):
        even, odd = 2 * pair, 2 * pair + 1
        step = jnp.concatenate([step_ref[source_of(even), :48, :], none], axis=1) + pltpu.roll(
            jnp.concatenate([step_ref[source_of(odd), :48, :], none], axis=1), HEAD, 1
        )
        columns = slice(pair * 384, (pair + 1) * 384)
        sq_ref[:, columns] = step
        factor = jnp.where(
            lane < HEAD,
            jnp.where(lane < NOPE, thrice(root[even : even + 1]), thrice(gamma[even : even + 1])),
            jnp.where(
                lane < HEAD + NOPE, thrice(root[odd : odd + 1]), thrice(gamma[odd : odd + 1])
            ),
        )
        nq_ref[:, columns] = (wq_ref[:, columns].astype(F32) * keep - LEARN_RATE * step) * factor
    for head in range(8):
        columns = slice(head * 128, (head + 1) * 128)
        step = step_ref[source_of(head), 48:, :128]
        sk_ref[:, columns] = step
        nk_ref[:, columns] = (
            wk_ref[:, columns].astype(F32) * keep - LEARN_RATE * step
        ) * root[head : head + 1]


def update(steps, owned_query, owned_key, flags):
    shapes = ((48, QR), (16, 1024), (48, QR), (16, 1024), (1, 8))
    return pl.pallas_call(
        update_kernel,
        out_shape=tuple(jax.ShapeDtypeStruct(shape, F32) for shape in shapes),
        in_specs=[VMEM] * 3 + [SMEM],
        out_specs=tuple(VMEM for _ in shapes),
        compiler_params=pltpu.CompilerParams(vmem_limit_bytes=16 * 2**20),
        cost_estimate=pl.CostEstimate(flops=1000, bytes_accessed=1000, transcendentals=0),
        name="update",
    )(steps, owned_query, owned_key, flags)


def turn_tables(positions):
    frequency = ROPE_THETA ** (-2.0 * jnp.arange(ROPE // 2, dtype=F32) / ROPE)
    angles = positions.astype(F32)[:, None] * frequency[None, :]
    cosine, sine = jnp.cos(angles), jnp.sin(angles)
    none = jnp.zeros_like(cosine)
    return (
        jnp.concatenate([cosine, cosine, none, none], axis=1),
        jnp.concatenate([-sine, none, none, none], axis=1),
        jnp.concatenate([none, sine, none, none], axis=1),
    )


def look_up(table, index):
    hit = index[:, None] == jnp.arange(table.shape[0], dtype=jnp.int32)[None, :]
    return jnp.sum(jnp.where(hit, table[None, :], 0), axis=1)


def shards(
    q_latent,
    kv_latent,
    key_rope,
    block_order,
    w_query,
    w_key,
    w_value,
    grad_query,
    grad_key,
    mom_query,
    mom_key,
    clip_flags,
):
    z, x, c = lax.axis_index("z"), lax.axis_index("x"), lax.axis_index("c")
    yl, yh = lax.axis_index("yl"), lax.axis_index("yh")
    ctx = z * 8 + x * 2 + yl
    rows_in = jnp.concatenate(
        [q_latent, kv_latent, key_rope, jnp.zeros((64, 64), BF16)], axis=1
    )
    key_rows = rows_in[:, QR:]
    flips = [rows_in] + [flip(rows_in, k) for k in (1, 2, 3)]
    swapped = [swap_core(piece) for piece in flips]

    def other_half(first, second):
        def pick(array):
            width = array.shape[1] // 2
            return jnp.where(yl == 0, array[:, width:], array[:, :width])

        return pick(first), pick(second)

    g_other = jnp.concatenate(other_half(grad_query, grad_key), axis=1)
    g_other = lax.ppermute(g_other, "yl", [(0, 1), (1, 0)])
    mom_q, mom_k = other_half(mom_query, mom_key)
    m_other = jnp.concatenate([mom_q, jnp.pad(mom_k, ((0, 0), (0, 256)))], axis=0)
    m_other = lax.ppermute(m_other, "yl", [(0, 1), (1, 0)])
    plane = lax.all_to_all(
        jnp.broadcast_to(key_rows[None], (16, 64, WIDE)), ("z", "x"), 0, 0
    )
    near = [flip(plane[:8], 1), flip(plane[:8], 3), flip(plane[8:], 1), flip(plane[8:], 3)]
    at = jnp.stack([c, z, x, yl, yh]).astype(jnp.int32)
    terms, l_own = gradient_terms(
        at, grad_query, grad_key, g_other, mom_query, mom_key, m_other, flips + swapped, []
    )
    terms = exchange(terms, FIRST)
    local_rows = jnp.arange(256, dtype=jnp.int32)
    qpos = look_up(block_order, 2 * ctx + jnp.arange(2, dtype=jnp.int32))
    query_pos = jnp.where(local_rows < 128, qpos[0], qpos[1]) * 128 + local_rows % 128
    wide = project_queries(l_own, w_query, w_key, *turn_tables(query_pos))
    far = [flip(near[1], 1), flip(near[2], 3)]
    mine = [plane, *near, *far]
    pieces = mine + [swap_core(piece) for piece in mine]
    slot = jnp.arange(16, dtype=jnp.int32)
    place = jnp.concatenate(
        [
            look_up(
                block_order,
                2 * (slot // 4 * 8 + slot % 4 * 2 + (yl ^ (k & 1))) + (yh ^ (k >> 1)),
            )
            for k in (0, 1, 3, 2)
        ]
    )
    place = jnp.concatenate([place[:24], place[32:40], place[24:32], place[40:]])
    core_rows = jnp.stack([c * 64, 64 - c * 64]).astype(jnp.int32)

    terms = sum_first(terms, [])
    parts = exchange(terms, SECOND)
    attn_out, peaks = attention(
        0, 8, place, core_rows, qpos, wide, w_value, pieces, [mark_after([*near, wide])]
    )
    moment, gram = moment_and_gram(parts, peaks)
    grams = [gram] + [move_z(gram, k) for k in (1, 2, 3)]
    steps = newton(moment, grams, [])
    steps = lax.all_to_all(steps, ("x", "yl"), 0, 0)
    step_query, step_key, new_query, new_key, head_peaks = update(
        steps,
        lax.dynamic_slice_in_dim(w_query, ctx * 48, 48, 0),
        lax.dynamic_slice_in_dim(w_key, ctx * 16, 16, 0),
        clip_flags,
    )
    return (attn_out, head_peaks.reshape(8), step_query, step_key, new_query, new_key)


def solution(mesh):
    fine = Mesh(mesh.devices.reshape(4, 4, 2, 2, 2), ("z", "x", "yl", "yh", "c"))
    ctx, dp = ("z", "x", "yl"), ("yh", "c")
    tokens = P(ctx + dp, None)
    columns = P(None, dp)
    both = P(ctx, dp)
    in_specs = (
        tokens,
        tokens,
        tokens,
        P(),
        columns,
        columns,
        columns,
        both,
        both,
        both,
        both,
        P(dp),
    )
    out_specs = (both, P(dp), both, both, both, both)
    return jax.shard_map(shards, mesh=fine, in_specs=in_specs, out_specs=out_specs, check_vma=False)
```
